256 devices in a mesh: dp: 2 (over x_hi), fsdp: 16 (over x_lo, y, core), tensor: 8 (over z).
Axes of the slice: x: 4 (x_hi: 2, x_lo: 2; x = x_hi * 2 + x_lo), y: 4, z: 8, core: 2. Of those that a mesh axis runs over, the one named last changes fastest.
Arguments:
- residual_input: bfloat16 [2, 512, 16384], P('dp', 'tensor', 'fsdp'), may hold values from -6 to 6
- block_output_gradient: bfloat16 [2, 512, 16384], P('dp', 'tensor', 'fsdp'), may hold values from -6 to 6
- norm_gain_vector: float32 [16384], P('fsdp'), may hold values from 0.5 to 1.5
- query_matrix: bfloat16 [16384, 8, 2048], P('fsdp', 'tensor'), may hold values from -0.046875 to 0.046875
- keyvalue_matrix: bfloat16 [16384, 2, 1024], P('fsdp', None, 'tensor'), may hold values from -0.046875 to 0.046875
- output_matrix: bfloat16 [8, 2048, 16384], P('tensor', None, 'fsdp'), may hold values from -0.046875 to 0.046875
- adapter_projection_down: bfloat16 [16384, 192], P('fsdp'), may hold values from -0.046875 to 0.046875
- adapter_query_up: bfloat16 [64, 8, 2048], P(None, 'tensor', 'fsdp'), may hold values from -0.75 to 0.75
- adapter_keyvalue_up: bfloat16 [64, 2, 1024], P(None, None, 'tensor'), may hold values from -0.75 to 0.75
- adapter_output_down: bfloat16 [8, 2048, 64], P('tensor', 'fsdp'), may hold values from -0.046875 to 0.046875
- adapter_output_up: bfloat16 [64, 16384], P(None, 'fsdp'), may hold values from -0.75 to 0.75
Outputs:
- grad_hidden: float32 [2, 512, 16384], P('dp', 'tensor', 'fsdp')
- projection_down_gradient: float32 [16384, 192], P('fsdp')
- query_up_gradient: float32 [64, 8, 2048], P(None, 'tensor', 'fsdp')
- keyvalue_up_gradient: float32 [64, 2, 1024], P(None, None, 'tensor')
- output_down_gradient: float32 [8, 2048, 64], P('tensor', 'fsdp')
- output_up_gradient: float32 [64, 16384], P(None, 'fsdp')
The draws below stay inside these ranges and needn't reach their ends.
All inputs are finite; a program needn't handle non-finite values.
Results may differ from the reference program's by a relative error of at most 0.025.
The reference program's roundings to bfloat16 on the way count: a program that leaves them out, or rounds other values in their place, can miss the bound.
Values may be sent and summed in bfloat16 or wider, within the bound.
A program may use at most 64 MiB of HBM per device.

```python
import math
import jax
import jax.numpy as jnp
from jax import lax

MODEL_WIDTH_SIZE = 16384
HEAD_SIZE = 128
ADAPTER_RANK = 64
SEQ = 512
KEYVALUE_HEADS = 8
GROUP_HEADS = 16
QUERY_HEADS = 128
BATCH = 2


def steps_of(stream_key, extent, shards, least, high):
    def one(position, shards_of):
        draws = jax.random.uniform(jax.random.fold_in(jax.random.fold_in(stream_key, 6), position), (shards_of,), jnp.float32, least / len(shards), high / len(shards))
        return jnp.repeat(jnp.exp(draws), extent[position] // shards_of).reshape((-1,) + (1,) * (len(extent) - position - 1))

    loudness = one(*shards[0])
    for cut in shards[1:]:
        loudness = loudness * one(*cut)
    return loudness


def centred(key, extent, spread, most, cuts=(), kind=jnp.bfloat16):
    array = jax.random.normal(key, extent, jnp.float32) * spread
    if len(cuts) > 0:
        array = steps_of(key, extent, cuts, -0.22, 0.18) * array
    return jnp.clip(array, min=-most, max=most).astype(kind)


def setup_inputs(seed: int = 0) -> dict:
    arg_keys = jax.random.split(jax.random.key(seed), 12)
    residual_input = centred(arg_keys[0], (BATCH, SEQ, MODEL_WIDTH_SIZE), 1.0, 6.0, ((0, 2), (1, 8), (2, 16)))
    block_output_gradient = centred(arg_keys[1], (BATCH, SEQ, MODEL_WIDTH_SIZE), 1.0, 6.0, ((0, 2), (1, 8), (2, 16)))
    norm_gain_vector = jnp.clip(1.0 + 0.1 * jax.random.normal(arg_keys[2], (MODEL_WIDTH_SIZE,), jnp.float32), 0.5, 1.5)
    query_matrix = centred(arg_keys[3], (MODEL_WIDTH_SIZE, KEYVALUE_HEADS, GROUP_HEADS * HEAD_SIZE), MODEL_WIDTH_SIZE ** -0.5, 0.046875, ((0, 16), (1, 8)))
    keyvalue_matrix = centred(arg_keys[4], (MODEL_WIDTH_SIZE, 2, KEYVALUE_HEADS * HEAD_SIZE), MODEL_WIDTH_SIZE ** -0.5, 0.046875, ((0, 16), (2, 8)))
    output_matrix = centred(arg_keys[5], (KEYVALUE_HEADS, GROUP_HEADS * HEAD_SIZE, MODEL_WIDTH_SIZE), (QUERY_HEADS * HEAD_SIZE) ** -0.5, 0.046875, ((0, 8), (2, 16)))
    adapter_projection_down = centred(arg_keys[6], (MODEL_WIDTH_SIZE, 3 * ADAPTER_RANK), MODEL_WIDTH_SIZE ** -0.5, 0.046875, ((0, 16),))
    adapter_query_up = centred(arg_keys[7], (ADAPTER_RANK, KEYVALUE_HEADS, GROUP_HEADS * HEAD_SIZE), ADAPTER_RANK ** -0.5, 0.75, ((1, 8), (2, 16)))
    adapter_keyvalue_up = centred(arg_keys[8], (ADAPTER_RANK, 2, KEYVALUE_HEADS * HEAD_SIZE), ADAPTER_RANK ** -0.5, 0.75, ((2, 8),))
    adapter_output_down = centred(arg_keys[9], (KEYVALUE_HEADS, GROUP_HEADS * HEAD_SIZE, ADAPTER_RANK), (QUERY_HEADS * HEAD_SIZE) ** -0.5, 0.046875, ((0, 8), (1, 16)))
    adapter_output_up = centred(arg_keys[10], (ADAPTER_RANK, MODEL_WIDTH_SIZE), ADAPTER_RANK ** -0.5, 0.75, ((1, 16),))
    return dict(residual_input=residual_input, block_output_gradient=block_output_gradient, norm_gain_vector=norm_gain_vector, query_matrix=query_matrix, keyvalue_matrix=keyvalue_matrix, output_matrix=output_matrix, adapter_projection_down=adapter_projection_down, adapter_query_up=adapter_query_up, adapter_keyvalue_up=adapter_keyvalue_up, adapter_output_down=adapter_output_down, adapter_output_up=adapter_output_up)


eps = 1e-05
adapter_scale = 2.0
theta = 500000.0

def rope_tables(length, width_total):
    half = width_total // 2
    freq = theta ** (-(jnp.arange(half, dtype=jnp.float32) * 2.0) / width_total)
    angles = jnp.arange(length, dtype=jnp.float32)[:, None] * freq[None, :]
    return (jnp.cos(angles), jnp.sin(angles))

def rotate(value_rows, cosine, sine):
    half = value_rows.shape[-1] // 2
    first = value_rows[..., :half]
    second = value_rows[..., half:]
    return jnp.concatenate([first * cosine - second * sine, second * cosine + first * sine], axis=-1)

def rotate_back(grads, cosine, sine):
    half = grads.shape[-1] // 2
    first = grads[..., :half]
    second = grads[..., half:]
    return jnp.concatenate([first * cosine + second * sine, second * cosine - first * sine], axis=-1)

def matrix_product(left, right):
    return jnp.dot(left, right, preferred_element_type=jnp.float32)

def reference(residual_input, block_output_gradient, norm_gain_vector, query_matrix, keyvalue_matrix, output_matrix, adapter_projection_down, adapter_query_up, adapter_keyvalue_up, adapter_output_down, adapter_output_up):
    single_float_type = jnp.float32
    brain_float_type = jnp.bfloat16
    query_weight_matrix = query_matrix.reshape(MODEL_WIDTH_SIZE, QUERY_HEADS * HEAD_SIZE)
    key_weight_matrix = keyvalue_matrix[:, 0, :]
    value_weight_matrix = keyvalue_matrix[:, 1, :]
    output_weight_matrix = output_matrix.reshape(QUERY_HEADS * HEAD_SIZE, MODEL_WIDTH_SIZE)
    query_up_weight = adapter_query_up.reshape(ADAPTER_RANK, QUERY_HEADS * HEAD_SIZE)
    key_up_weight = adapter_keyvalue_up[:, 0, :]
    value_up_weight = adapter_keyvalue_up[:, 1, :]
    output_down_weight = adapter_output_down.reshape(QUERY_HEADS * HEAD_SIZE, ADAPTER_RANK)
    cosine, sine = rope_tables(SEQ, HEAD_SIZE)
    cos3 = cosine[:, None, :]
    sin3 = sine[:, None, :]
    causal = jnp.arange(SEQ)[:, None] >= jnp.arange(SEQ)[None, :]
    scale = 1.0 / math.sqrt(HEAD_SIZE)
    projection_down_total = jnp.zeros((MODEL_WIDTH_SIZE, 3 * ADAPTER_RANK), single_float_type)
    query_up_total = jnp.zeros((ADAPTER_RANK, QUERY_HEADS * HEAD_SIZE), single_float_type)
    keyvalue_up_total = jnp.zeros((ADAPTER_RANK, 2, KEYVALUE_HEADS * HEAD_SIZE), single_float_type)
    output_down_total = jnp.zeros((QUERY_HEADS * HEAD_SIZE, ADAPTER_RANK), single_float_type)
    output_up_total = jnp.zeros((ADAPTER_RANK, MODEL_WIDTH_SIZE), single_float_type)
    gradient_listing = []
    for batch in range(BATCH):
        hidden_gathered = residual_input[batch].astype(single_float_type)
        inverse_deviation = lax.rsqrt(lax.optimization_barrier(jnp.mean(hidden_gathered * hidden_gathered, axis=-1, keepdims=True)) + eps)
        hidden_normalized = hidden_gathered * inverse_deviation
        normed_hidden = (hidden_normalized * norm_gain_vector).astype(brain_float_type)
        lowrank_input = matrix_product(normed_hidden, adapter_projection_down).astype(brain_float_type)
        lowrank_query = lowrank_input[:, :ADAPTER_RANK]
        lowrank_key = lowrank_input[:, ADAPTER_RANK:2 * ADAPTER_RANK]
        lowrank_value = lowrank_input[:, 2 * ADAPTER_RANK:]
        query_rows = matrix_product(normed_hidden, query_weight_matrix) + adapter_scale * matrix_product(lowrank_query, query_up_weight)
        key_rows = matrix_product(normed_hidden, key_weight_matrix) + adapter_scale * matrix_product(lowrank_key, key_up_weight)
        value_rows = matrix_product(normed_hidden, value_weight_matrix) + adapter_scale * matrix_product(lowrank_value, value_up_weight)
        qrot = rotate(query_rows.reshape(SEQ, QUERY_HEADS, HEAD_SIZE), cos3, sin3).astype(brain_float_type)
        krot = rotate(key_rows.reshape(SEQ, KEYVALUE_HEADS, HEAD_SIZE), cos3, sin3).astype(brain_float_type)
        vals = value_rows.reshape(SEQ, KEYVALUE_HEADS, HEAD_SIZE).astype(brain_float_type)
        kwide = jnp.repeat(krot, GROUP_HEADS, axis=1).astype(single_float_type)
        vwide = jnp.repeat(vals, GROUP_HEADS, axis=1).astype(single_float_type)
        scores = jnp.einsum('qhd,khd->hqk', qrot.astype(single_float_type), kwide) * scale
        scores = jnp.where(causal[None], scores, -1e+30)
        probs = jax.nn.softmax(scores, axis=-1)
        probs_b = probs.astype(brain_float_type)
        attention_output = jnp.einsum('hqk,khd->qhd', probs_b.astype(single_float_type), vwide).astype(brain_float_type)
        attention_rows = attention_output.reshape(SEQ, QUERY_HEADS * HEAD_SIZE)
        output_gradient = block_output_gradient[batch]
        lowrank_output = matrix_product(attention_rows, output_down_weight).astype(brain_float_type)
        backward_output = matrix_product(output_gradient, adapter_output_up.T).astype(brain_float_type)
        output_up_total = output_up_total + adapter_scale * matrix_product(lowrank_output.T, output_gradient)
        output_down_total = output_down_total + adapter_scale * matrix_product(attention_rows.T, backward_output)
        attention_gradient = (matrix_product(output_gradient, output_weight_matrix.T) + adapter_scale * matrix_product(backward_output, output_down_weight.T)).astype(brain_float_type)
        attention_gradient = attention_gradient.reshape(SEQ, QUERY_HEADS, HEAD_SIZE).astype(single_float_type)
        dprobs = jnp.einsum('qhd,khd->hqk', attention_gradient, vwide)
        dval = jnp.einsum('hqk,qhd->khd', probs_b.astype(single_float_type), attention_gradient)
        dval = dval.reshape(SEQ, KEYVALUE_HEADS, GROUP_HEADS, HEAD_SIZE).sum(axis=2)
        delta = lax.optimization_barrier(jnp.sum(probs * dprobs, axis=-1, keepdims=True))
        dscore = (probs * (dprobs - delta) * scale).astype(brain_float_type).astype(single_float_type)
        dquery = jnp.einsum('hqk,khd->qhd', dscore, kwide)
        dkey = jnp.einsum('hqk,qhd->khd', dscore, qrot.astype(single_float_type)).reshape(SEQ, KEYVALUE_HEADS, GROUP_HEADS, HEAD_SIZE).sum(axis=2)
        query_gradient = rotate_back(dquery, cos3, sin3).astype(brain_float_type).reshape(SEQ, QUERY_HEADS * HEAD_SIZE)
        key_gradient = rotate_back(dkey, cos3, sin3).astype(brain_float_type).reshape(SEQ, KEYVALUE_HEADS * HEAD_SIZE)
        value_gradient = dval.astype(brain_float_type).reshape(SEQ, KEYVALUE_HEADS * HEAD_SIZE)
        backward_input = jnp.concatenate([matrix_product(query_gradient, query_up_weight.T), matrix_product(key_gradient, key_up_weight.T), matrix_product(value_gradient, value_up_weight.T)], axis=1).astype(brain_float_type)
        projection_down_total = projection_down_total + adapter_scale * matrix_product(normed_hidden.T, backward_input)
        query_up_total = query_up_total + adapter_scale * matrix_product(lowrank_query.T, query_gradient)
        keyvalue_up_total = keyvalue_up_total + adapter_scale * jnp.stack([matrix_product(lowrank_key.T, key_gradient), matrix_product(lowrank_value.T, value_gradient)], axis=1)
        normed_gradient = matrix_product(query_gradient, query_weight_matrix.T) + matrix_product(key_gradient, key_weight_matrix.T) + matrix_product(value_gradient, value_weight_matrix.T) + adapter_scale * matrix_product(backward_input, adapter_projection_down.T)
        normalized_gradient = normed_gradient * norm_gain_vector
        inner_product = lax.optimization_barrier(jnp.mean(normalized_gradient * hidden_normalized, axis=-1, keepdims=True))
        gradient_listing.append(output_gradient.astype(single_float_type) + inverse_deviation * (normalized_gradient - hidden_normalized * inner_product))
    grad_hidden = jnp.stack(gradient_listing, axis=0)
    return (grad_hidden, projection_down_total, query_up_total.reshape(ADAPTER_RANK, KEYVALUE_HEADS, GROUP_HEADS * HEAD_SIZE), keyvalue_up_total, output_down_total.reshape(KEYVALUE_HEADS, GROUP_HEADS * HEAD_SIZE, ADAPTER_RANK), output_up_total)
```

```python
import math

import jax
import jax.numpy as jnp
import numpy as np
from jax import lax
from jax.experimental import pallas as pl
from jax.experimental.pallas import tpu as pltpu
from jax.sharding import PartitionSpec as P

eps = 1e-05
adapter_scale = 2.0
theta = 500000.0
MESH = pl.DeviceIdType.MESH
F32 = jnp.float32
BF16 = jnp.bfloat16

NF = 16
NC = 8
NT = 8
L = 512
T = 64
W = 1024
H = 128
R = 32


def rope_tables():
    half = H // 2
    freq = np.float32(theta) ** (-(np.arange(half, dtype=np.float32) * np.float32(2.0)) / np.float32(H))
    angles = np.arange(L, dtype=np.float32)[:, None] * freq[None, :].astype(np.float32)
    angles = angles.astype(np.float64)
    cosine, sine = np.cos(angles), np.sin(angles)
    return (
        np.concatenate([cosine, cosine], axis=1).astype(np.float32),
        np.concatenate([-sine, sine], axis=1).astype(np.float32),
    )


def dot(a, b, ca, cb, **kw):
    return lax.dot_general(a, b, (((ca,), (cb,)), ((), ())), preferred_element_type=F32, **kw)


def rotate(v, c, s):
    return v * c + pltpu.roll(v, H // 2, axis=1) * s


def rotate_back(v, c, s):
    return v * c - pltpu.roll(v, H // 2, axis=1) * s


def kernel(
    x_h, g_h, gain_h, wq_h, wo_h, wkv_h, dwt_h, gup_h, ups_h, odt_h, cos_h, sin_h,
    hid_o, pd_o, ou_o, sm_o,
    xb, gb, nb, wq, wo, wkv, dwt, gup, upq, upk, upv, odt, odb, gain, cosb, sinb,
    ss_own, ss_recv, r_all, ip_own, ip_recv,
    bo_part, bo_recv, bo_all, kvl_part, kvl_recv, kvl_all,
    a_acc, a_pair, a_precv, a_send, a_recv,
    q_acc, q_pair, q_precv, q_send, q_recv,
    dq_all, qrot, dat, attn, dkacc,
    p1_part, p1_recv, dkv_all, p2_all, back_all,
    zpart, rs_sendr, rs_recvr, rs_sendl, rs_recvl,
    sm_own, sm_recv, sl_own, sl_recv, sl_all,
    ld, grp_s, grp_r, ring_s, ring_r, pair_s, pair_r, chip_s, chip_r, rs_s, rs_r, dp_s, dp_r,
):
    d = lax.axis_index("dp")
    f = lax.axis_index("fsdp")
    t = lax.axis_index("tensor")
    c = f // 2
    k = f % 2

    def rcopy(src, dst, ss, rs, dev):
        return pltpu.make_async_remote_copy(
            src_ref=src, dst_ref=dst, send_sem=ss, recv_sem=rs, device_id=dev, device_id_type=MESH
        )

    def wait_bytes(ref, sem):
        pltpu.make_async_copy(ref, ref, sem).wait()

    def fdev(i):
        return (d, lax.rem(f + i, NF), t)

    def zdev(i):
        return (d, f, lax.rem(t + i + NT, NT))

    loads = [
        (x_h, xb.at[pl.ds(pl.multiple_of(t * T, T), T)]),
        (g_h, gb.at[pl.ds(pl.multiple_of(t * T, T), T)]),
        (gain_h, gain),
        (wo_h, wo),
        (wq_h, wq),
        (wkv_h, wkv),
        (dwt_h, dwt.at[pl.ds(0, 192)]),
        (gup_h, gup.at[pl.ds(0, 64)]),
        (ups_h.at[pl.ds(0, 64)], upq.at[pl.ds(0, 64)]),
        (ups_h.at[pl.ds(64, 64)], upk.at[pl.ds(64, 64)]),
        (ups_h.at[pl.ds(128, 64)], upv.at[pl.ds(128, 64)]),
        (odt_h, odt.at[pl.ds(0, 64)]),
        (odt_h, odb.at[pl.ds(192, 64)]),
        (cos_h, cosb),
        (sin_h, sinb),
    ]
    copies = [pltpu.make_async_copy(s, o, ld.at[i]) for i, (s, o) in enumerate(loads)]
    for copy in copies:
        copy.start()

    barrier = pltpu.get_barrier_semaphore()

    @pl.loop(1, NF)
    def _(i):
        pl.semaphore_signal(barrier, inc=1, device_id=fdev(i), device_id_type=MESH)

    @pl.loop(1, NT)
    def _(i):
        pl.semaphore_signal(barrier, inc=1, device_id=zdev(i), device_id_type=MESH)

    other = (1 - d, f, t)
    pl.semaphore_signal(barrier, inc=1, device_id=other, device_id_type=MESH)

    dwt[pl.ds(192, 64)] = jnp.zeros((64, W), BF16)
    gup[pl.ds(64, 64)] = jnp.zeros((64, W), BF16)
    upq[pl.ds(64, 192)] = jnp.zeros((192, H), BF16)
    upk[pl.ds(0, 64)] = jnp.zeros((64, H), BF16)
    upk[pl.ds(128, 128)] = jnp.zeros((128, H), BF16)
    upv[pl.ds(0, 128)] = jnp.zeros((128, H), BF16)
    upv[pl.ds(192, 64)] = jnp.zeros((64, H), BF16)
    odt[pl.ds(64, 64)] = jnp.zeros((64, H), BF16)
    odb[pl.ds(0, 192)] = jnp.zeros((192, H), BF16)

    pl.semaphore_wait(barrier, NF - 1 + NT - 1 + 1)

    def ring(buf, rows, n):
        def piece(z, off, size):
            return buf.at[pl.ds(pl.multiple_of(lax.rem(t + z + 2 * NT, NT) * rows + off, 16), size)]

        def right(s):
            ref = piece(1 - s, 0, rows if s < 4 else rows // 2)
            return rcopy(ref, ref, ring_s.at[n, 0, s - 1], ring_r.at[n, 0, s - 1], zdev(1))

        def left(s):
            ref = piece(s - 1, 0, rows) if s < 4 else piece(3, rows // 2, rows // 2)
            return rcopy(ref, ref, ring_s.at[n, 1, s - 1], ring_r.at[n, 1, s - 1], zdev(-1))

        def start(s):
            right(s).start()
            left(s).start()

        def arrive(s):
            right(s).wait_recv()
            left(s).wait_recv()

        def finish():
            for s in range(1, 5):
                right(s).wait_send()
                left(s).wait_send()

        return start, arrive, finish

    g_start, g_arrive, g_finish = ring(gb, T, 0)
    x_start, x_arrive, x_finish = ring(xb, T, 1)
    sl_start, sl_arrive, sl_finish = ring(sl_all, 256, 2)

    def scatter_f(src, rows, recv, n):
        @pl.loop(1, NF)
        def _(i):
            fi = lax.rem(f + i, NF)
            rcopy(
                src.at[pl.ds(pl.multiple_of(fi * rows, rows), rows)],
                recv.at[i - 1],
                grp_s.at[n],
                grp_r.at[n],
                (d, fi, t),
            ).start()

    def gather_f(buf, rows, n):
        ref = buf.at[pl.ds(pl.multiple_of(f * rows, rows), rows)]

        @pl.loop(1, NF)
        def _(i):
            rcopy(ref, ref, grp_s.at[n], grp_r.at[n], fdev(i)).start()

    def total_f(own, recv):
        def add(i, total):
            return total + recv[i].astype(F32)

        return lax.fori_loop(0, NF - 1, add, own.astype(F32))

    copies[1].wait()
    g_start(1)
    copies[0].wait()

    own_rows = pl.ds(pl.multiple_of(t * T, T), T)
    ones = jnp.ones((8, W), F32)

    def column(rows8):
        return rows8.T[:T, 0:1]

    x_own = xb[own_rows].astype(F32)
    squares = dot(ones, x_own * x_own, 1, 1, precision=lax.Precision.HIGHEST)
    ss_own[...] = jnp.concatenate([squares, squares], axis=1)

    @pl.loop(1, NF)
    def _(i):
        rcopy(ss_own, ss_recv.at[i - 1], grp_s.at[0], grp_r.at[0], fdev(i)).start()

    g_arrive(1)
    g_start(2)
    x_start(1)
    wait_bytes(ss_recv, grp_r.at[0])
    squares = total_f(ss_own[...], ss_recv)
    r_all[t] = lax.rsqrt(squares / (W * NF) + eps)

    @pl.loop(1, NT)
    def _(i):
        rcopy(r_all.at[t], r_all.at[t], grp_s.at[1], grp_r.at[1], zdev(i)).start()

    copies[2].wait()

    def normalise(z):
        z = lax.rem(t + z + NT, NT)
        rows = pl.ds(pl.multiple_of(z * T, T), T)
        nb[rows] = (xb[rows].astype(F32) * column(r_all[z]) * gain[...]).astype(BF16)

    g_arrive(2)
    g_start(3)
    g_arrive(3)
    g_start(4)
    wait_bytes(r_all.at[pl.ds(0, NT - 1)], grp_r.at[1])
    normalise(0)
    copies[3].wait()
    copies[7].wait()
    g_arrive(4)

    bo_part[...] = dot(gb[...], gup[...], 1, 1).astype(BF16)
    scatter_f(bo_part, R, bo_recv, 2)

    mate = (d, 2 * c + 1 - k, t)

    def chip_at(i):
        return lax.rem(c + 1 + i, NC)

    def heads(product, acc, pair, precv, send, recv, n, extra):
        def pair_copy(i):
            return rcopy(pair.at[i], precv.at[i], pair_s.at[n, i], pair_r.at[n, i], mate)

        def chip_copy(i):
            dev = (d, 2 * chip_at(i) + k, t)
            return rcopy(send.at[i], recv.at[i], chip_s.at[n, i], chip_r.at[n, i], dev)

        def second(i):
            pair_copy(i).wait_recv()
            send[i] = (acc[i] + precv[i].astype(F32)).astype(BF16)
            chip_copy(i).start()

        @pl.loop(0, NC)
        def _(i):
            both = product(chip_at(i))
            acc[i] = jnp.where(k == 0, both[:, :H], both[:, H:])
            pair[i] = jnp.where(k == 0, both[:, H:], both[:, :H]).astype(BF16)
            pair_copy(i).start()

            @pl.when(i > 0)
            def _():
                second(i - 1)

            extra(i)

        pair_copy(NC - 1).wait_recv()

        def total():
            def add(i, value):
                chip_copy(i).wait_recv()
                return value + recv[i].astype(F32)

            return lax.fori_loop(0, NC - 1, add, acc[NC - 1] + precv[NC - 1].astype(F32))

        def finish():
            @pl.loop(0, NC)
            def _(i):
                pair_copy(i).wait_send()

            @pl.loop(0, NC - 1)
            def _(i):
                chip_copy(i).wait_send()

        return total, finish

    def a_product(ci):
        return dot(gb[...], wo[pl.ds(pl.multiple_of(ci * 256, 256), 256), :], 1, 1)

    def a_extra(i):
        for s in range(1, 4):

            @pl.when(i == 2 * s - 1)
            def _(s=s):
                x_arrive(s)
                x_start(s + 1)
                normalise(-s)
                normalise(s)

    a_total, a_finish = heads(a_product, a_acc, a_pair, a_precv, a_send, a_recv, 0, a_extra)

    wait_bytes(bo_recv, grp_r.at[2])
    own_piece = pl.ds(pl.multiple_of(f * R, R), R)
    bo_all[own_piece] = total_f(bo_part[own_piece], bo_recv).astype(BF16)
    gather_f(bo_all, R, 3)

    x_arrive(4)
    normalise(4)

    copies[5].wait()
    copies[6].wait()

    @pl.loop(0, 4)
    def _(i):
        rows = pl.ds(pl.multiple_of(i * 128, 128), 128)
        kvl_part[rows, pl.ds(0, 256)] = dot(nb[rows], wkv[...], 1, 0).astype(BF16)
        kvl_part[rows, pl.ds(256, 256)] = dot(nb[rows], dwt[...], 1, 1).astype(BF16)

    scatter_f(kvl_part, R, kvl_recv, 4)
    copies[4].wait()
    for i in range(8, 15):
        copies[i].wait()

    def q_product(ci):
        return dot(nb[...], wq[:, pl.ds(pl.multiple_of(ci * 256, 256), 256)], 1, 0)

    def q_extra(i):
        @pl.when(i == 4)
        def _():
            wait_bytes(kvl_recv, grp_r.at[4])
            total = total_f(kvl_part[own_piece], kvl_recv)
            low = total[:, 256:].astype(BF16)
            keys = total[:, :H] + adapter_scale * dot(low, upk[...], 1, 0)
            values = total[:, H:256] + adapter_scale * dot(low, upv[...], 1, 0)
            keys = rotate(keys, cosb[own_piece], sinb[own_piece])
            kvl_all[own_piece, pl.ds(0, H)] = keys.astype(BF16)
            kvl_all[own_piece, pl.ds(H, H)] = values.astype(BF16)
            kvl_all[own_piece, pl.ds(256, 256)] = low
            gather_f(kvl_all, R, 5)

    q_total, q_finish = heads(q_product, q_acc, q_pair, q_precv, q_send, q_recv, 1, q_extra)

    gathered = pl.ds(0, (NF - 1) * R)
    wait_bytes(bo_all.at[gathered], grp_r.at[3])
    dat[...] = (a_total() + adapter_scale * dot(bo_all[...], odt[...], 1, 0)).astype(BF16)

    wait_bytes(kvl_all.at[gathered], grp_r.at[5])
    low_cols = pl.ds(256, 256)
    query = q_total() + adapter_scale * dot(kvl_all[:, low_cols], upq[...], 1, 0)
    qrot[...] = rotate(query, cosb[...], sinb[...]).astype(BF16)

    scale = 1.0 / math.sqrt(H)
    dkacc[...] = jnp.zeros_like(dkacc)
    dq_cols = pl.ds(pl.multiple_of(f * H, H), H)
    for i in range(4):
        rows = pl.ds(i * 128, 128)
        seen = pl.ds(0, (i + 1) * 128)
        n = (i + 1) * 128
        krot = kvl_all[seen, pl.ds(0, H)]
        vals = kvl_all[seen, pl.ds(H, H)]
        qi = qrot[rows]
        da = dat[rows]
        scores = dot(qi, krot, 1, 1) * scale
        causal = lax.broadcasted_iota(jnp.int32, (128, n), 0) + i * 128 >= lax.broadcasted_iota(
            jnp.int32, (128, n), 1
        )
        scores = jnp.where(causal, scores, -1e30)
        e = jnp.exp(scores - jnp.max(scores, axis=1, keepdims=True))
        probs = e / jnp.sum(e, axis=1, keepdims=True)
        probs_b = probs.astype(BF16)
        attn[rows] = dot(probs_b, vals, 1, 0).astype(BF16)
        dprobs = dot(da, vals, 1, 1)
        delta = jnp.sum(probs * dprobs, axis=1, keepdims=True)
        dscore = (probs * (dprobs - delta) * scale).astype(BF16)
        dquery = dot(dscore, krot, 1, 0)
        dq_all[rows, dq_cols] = rotate_back(dquery, cosb[rows], sinb[rows]).astype(BF16)
        dkacc[seen, pl.ds(0, H)] += dot(dscore, qi, 0, 0)
        dkacc[seen, pl.ds(H, H)] += dot(probs_b, da, 0, 0)

    def dq_ref(ci, core):
        return dq_all.at[:, pl.ds(pl.multiple_of((2 * ci + core) * H, H), H)]

    def dq_copy(i):
        ref = dq_ref(c, k)
        return rcopy(ref, ref, chip_s.at[2, i], chip_r.at[2, i], (d, 2 * chip_at(i) + k, t))

    def dq_forward(i):
        ref = dq_ref(lax.rem(c - 1 - i + 2 * NC, NC), k)
        return rcopy(ref, ref, pair_s.at[2, i + 1], pair_r.at[2, i + 1], mate)

    @pl.loop(0, NC - 1)
    def _(i):
        dq_copy(i).start()

    dq_forward(-1).start()

    dq_own = dq_all[:, dq_cols]
    p1_part[:, pl.ds(0, 256)] = dkacc[...].astype(BF16)
    p1_part[:, pl.ds(256, 256)] = (
        dot(dq_own, upq[...], 1, 1) + dot(attn[...], odb[...], 1, 1)
    ).astype(BF16)
    scatter_f(p1_part, R, p1_recv, 6)

    sm_own[pl.ds(0, 64)] = dot(kvl_all[:, low_cols], dq_own, 0, 0)[:64]
    sm_own[pl.ds(192, 64)] = dot(bo_all[...], attn[...], 0, 0)[:64]

    wait_bytes(p1_recv, grp_r.at[6])
    total = total_f(p1_part[own_piece], p1_recv)
    dkey = rotate_back(total[:, :H], cosb[own_piece], sinb[own_piece]).astype(BF16)
    dval = total[:, H:256].astype(BF16)
    dkv_all[own_piece, pl.ds(0, H)] = dkey
    dkv_all[own_piece, pl.ds(H, H)] = dval
    gather_f(dkv_all, R, 7)
    p2_all[t] = (total[:, 256:] + dot(dkey, upk[...], 1, 1) + dot(dval, upv[...], 1, 1)).astype(BF16)

    @pl.loop(1, NT)
    def _(i):
        rcopy(p2_all.at[t], p2_all.at[t], grp_s.at[8], grp_r.at[8], zdev(i)).start()

    @pl.loop(0, NC - 1)
    def _(i):
        dq_copy(i).wait_recv()
        dq_forward(i).start()

    wait_bytes(p2_all.at[pl.ds(0, NT - 1)], grp_r.at[8])
    total = p2_all[0].astype(F32)
    for i in range(1, NT):
        total = total + p2_all[i].astype(F32)
    back_all[own_piece] = total.astype(BF16)
    gather_f(back_all, R, 9)

    wait_bytes(dkv_all.at[gathered], grp_r.at[7])
    kv_up = dot(kvl_all[:, low_cols], dkv_all[...], 0, 0)
    sm_own[pl.ds(64, 64)] = kv_up[64:128, :H]
    sm_own[pl.ds(128, 64)] = kv_up[128:192, H:]
    small = rcopy(sm_own, sm_recv, dp_s.at[0], dp_r.at[0], other)
    small.start()

    @pl.loop(0, NC)
    def _(i):
        dq_forward(i - 1).wait_recv()

    def depth(j, way):
        return 4 if j % 2 == way else 3

    def rs_copy(j, way, s):
        send, recv = ((rs_sendr, rs_recvr), (rs_sendl, rs_recvl))[way]
        return rcopy(
            send.at[j, s - 1], recv.at[j, s - 1], rs_s.at[way, j, s - 1], rs_r.at[way, j, s - 1], zdev(1 - 2 * way)
        )

    def rs_step(j, way, s):
        hops = depth(j, way) - s + 1
        z = lax.rem(t + (hops if way == 0 else -hops) + NT, NT)
        value = zpart[j, pl.ds(pl.multiple_of(z * T, T), T)]
        send, recv = ((rs_sendr, rs_recvr), (rs_sendl, rs_recvl))[way]
        if s > 1:
            rs_copy(j, way, s - 1).wait_recv()
            value = value + recv[j, s - 2].astype(F32)
        send[j, s - 1] = value.astype(BF16)
        rs_copy(j, way, s).start()

    for w in range(4 + 3):
        if w < 4:
            rows = pl.ds(w * 256, 256)
            zpart[w] = dot(dq_all[...], wq[rows, :], 1, 1) + dot(dkv_all[...], wkv[rows, :], 1, 1)
        for j in range(min(w, 3), -1, -1):
            s = w - j + 1
            for way in range(2):
                if s <= depth(j, way):
                    rs_step(j, way, s)

    wait_bytes(back_all.at[gathered], grp_r.at[9])
    cols = pl.ds(pl.multiple_of(t * H, H), H)
    sl_own[pl.ds(0, 192)] = dot(back_all[...], nb[:, cols], 0, 0)[:192]
    sl_own[pl.ds(192, 64)] = dot(back_all[...], gb[:, cols], 0, 0)[192:]
    slices = rcopy(sl_own, sl_recv, dp_s.at[1], dp_r.at[1], other)
    slices.start()

    back_own = back_all[own_rows]
    inverse = column(r_all[t])
    xhat = x_own * inverse
    dhat = []
    for j in range(4):
        wide = pl.ds(j * 256, 256)
        for way in range(2):
            rs_copy(j, way, depth(j, way)).wait_recv()
        value = zpart[j, own_rows] + rs_recvr[j, depth(j, 0) - 1].astype(F32) + rs_recvl[j, depth(j, 1) - 1].astype(F32)
        value = value + adapter_scale * dot(back_own, dwt[:, wide], 1, 0)
        dhat.append(value * gain[:, wide])
    dhat = jnp.concatenate(dhat, axis=1)
    inner = dot(ones, dhat * xhat, 1, 1, precision=lax.Precision.HIGHEST)
    ip_own[...] = jnp.concatenate([inner, inner], axis=1)

    @pl.loop(1, NF)
    def _(i):
        rcopy(ip_own, ip_recv.at[i - 1], grp_s.at[10], grp_r.at[10], fdev(i)).start()

    slices.wait_recv()
    sl_all[pl.ds(pl.multiple_of(t * 256, 256), 256)] = (sl_own[...] + sl_recv[...]).astype(BF16)
    sl_start(1)

    small.wait_recv()
    sm_o[...] = sm_own[...] + sm_recv[...]

    wait_bytes(ip_recv, grp_r.at[10])
    inner = total_f(ip_own[...], ip_recv) / (W * NF)
    hid_o[...] = inverse * (dhat - xhat * column(inner))

    for s in range(1, 5):
        sl_arrive(s)
        if s < 4:
            sl_start(s + 1)
    for z in range(NT):
        piece = sl_all[pl.ds(z * 256, 256)].astype(F32)
        pd_o[:, pl.ds(z * H, H)] = piece[:192]
        ou_o[:, pl.ds(z * H, H)] = piece[192:]

    g_finish()
    x_finish()
    sl_finish()
    a_finish()
    q_finish()

    @pl.loop(0, NC - 1)
    def _(i):
        dq_copy(i).wait_send()

    @pl.loop(0, NC)
    def _(i):
        dq_forward(i - 1).wait_send()

    for j in range(4):
        for way in range(2):
            for s in range(1, depth(j, way) + 1):
                rs_copy(j, way, s).wait_send()
    small.wait_send()
    slices.wait_send()
    sent = [
        ss_recv, r_all.at[pl.ds(0, NT - 1)], bo_recv, bo_all.at[gathered], kvl_recv, kvl_all.at[gathered],
        p1_recv, dkv_all.at[gathered], p2_all.at[pl.ds(0, NT - 1)], back_all.at[gathered], ip_recv,
    ]
    for n, ref in enumerate(sent):
        wait_bytes(ref, grp_s.at[n])


def local(
    residual_input,
    block_output_gradient,
    norm_gain_vector,
    query_matrix,
    keyvalue_matrix,
    output_matrix,
    adapter_projection_down,
    adapter_query_up,
    adapter_keyvalue_up,
    adapter_output_down,
    adapter_output_up,
):
    cosine, sine = rope_tables()
    ups = jnp.concatenate(
        [adapter_query_up[:, 0, :], adapter_keyvalue_up[:, 0, :], adapter_keyvalue_up[:, 1, :]], axis=0
    )
    vm = pltpu.VMEM
    dma = pltpu.SemaphoreType.DMA
    chips = [
        vm((NC, L, H), F32),
        vm((NC, L, H), BF16),
        vm((NC, L, H), BF16),
        vm((NC - 1, L, H), BF16),
        vm((NC - 1, L, H), BF16),
    ]
    scratch = [
        vm((L, W), BF16), vm((L, W), BF16), vm((L, W), BF16),
        vm((W, 2048), BF16), vm((2048, W), BF16), vm((W, 256), BF16), vm((256, W), BF16), vm((128, W), BF16),
        vm((256, H), BF16), vm((256, H), BF16), vm((256, H), BF16), vm((128, H), BF16), vm((256, H), BF16),
        vm((1, W), F32), vm((L, H), F32), vm((L, H), F32),
        vm((8, H), F32), vm((NF - 1, 8, H), F32), vm((NT, 8, H), F32), vm((8, H), F32), vm((NF - 1, 8, H), F32),
        vm((L, H), BF16), vm((NF - 1, R, H), BF16), vm((L, H), BF16),
        vm((L, 512), BF16), vm((NF - 1, R, 512), BF16), vm((L, 512), BF16),
        *chips, *chips,
        vm((L, 2048), BF16), vm((L, H), BF16), vm((L, H), BF16), vm((L, H), BF16), vm((L, 256), F32),
        vm((L, 512), BF16), vm((NF - 1, R, 512), BF16), vm((L, 256), BF16), vm((NT, R, 256), BF16), vm((L, 256), BF16),
        vm((4, L, 256), F32),
        vm((4, 4, T, 256), BF16), vm((4, 4, T, 256), BF16), vm((4, 4, T, 256), BF16), vm((4, 4, T, 256), BF16),
        vm((256, H), F32), vm((256, H), F32), vm((256, H), F32), vm((256, H), F32), vm((NT * 256, H), BF16),
        dma((15,)), dma((11,)), dma((11,)), dma((3, 2, 4)), dma((3, 2, 4)),
        dma((3, NC)), dma((3, NC)), dma((3, NC)), dma((3, NC)), dma((2, 4, 4)), dma((2, 4, 4)),
        dma((2,)), dma((2,)),
    ]
    hidden, down, up, small = pl.pallas_call(
        kernel,
        out_shape=(
            jax.ShapeDtypeStruct((T, W), F32),
            jax.ShapeDtypeStruct((192, W), F32),
            jax.ShapeDtypeStruct((64, W), F32),
            jax.ShapeDtypeStruct((256, H), F32),
        ),
        in_specs=[pl.BlockSpec(memory_space=pl.ANY)] * 12,
        out_specs=(pl.BlockSpec(memory_space=pltpu.VMEM),) * 4,
        scratch_shapes=scratch,
        compiler_params=pltpu.CompilerParams(
            collective_id=0, has_side_effects=True, vmem_limit_bytes=60 * 2**20
        ),
        name="adapter_backward",
    )(
        residual_input[0],
        block_output_gradient[0],
        norm_gain_vector[None],
        query_matrix[:, 0, :],
        output_matrix[0],
        keyvalue_matrix.reshape(W, 256),
        adapter_projection_down.T,
        adapter_output_up,
        ups,
        adapter_output_down[0].T,
        jnp.asarray(cosine),
        jnp.asarray(sine),
    )
    hidden = block_output_gradient.astype(F32) + hidden[None]
    small = small * adapter_scale
    return (
        hidden,
        (down * adapter_scale).T,
        small[:64, None, :],
        jnp.stack([small[64:128], small[128:192]], axis=1),
        small[192:].T[None],
        up * adapter_scale,
    )


def solution(mesh):
    in_specs = (
        P("dp", "tensor", "fsdp"),
        P("dp", "tensor", "fsdp"),
        P("fsdp"),
        P("fsdp", "tensor", None),
        P("fsdp", None, "tensor"),
        P("tensor", None, "fsdp"),
        P("fsdp", None),
        P(None, "tensor", "fsdp"),
        P(None, None, "tensor"),
        P("tensor", "fsdp", None),
        P(None, "fsdp"),
    )
    out_specs = (
        P("dp", "tensor", "fsdp"),
        P("fsdp", None),
        P(None, "tensor", "fsdp"),
        P(None, None, "tensor"),
        P("tensor", "fsdp", None),
        P(None, "fsdp"),
    )
    return jax.shard_map(local, mesh=mesh, in_specs=in_specs, out_specs=out_specs, check_vma=False)
```

```python
import math

import jax
import jax.numpy as jnp
import numpy as np
from jax import lax
from jax.experimental import pallas as pl
from jax.experimental.pallas import tpu as pltpu
from jax.sharding import PartitionSpec as P

eps = 1e-05
adapter_scale = 2.0
theta = 500000.0
MESH = pl.DeviceIdType.MESH
F32 = jnp.float32
BF16 = jnp.bfloat16

NF = 16
NC = 8
NT = 8
L = 512
T = 64
W = 1024
H = 128
R = 32


def rope_tables():
    half = H // 2
    freq = np.float32(theta) ** (-(np.arange(half, dtype=np.float32) * np.float32(2.0)) / np.float32(H))
    angles = np.arange(L, dtype=np.float32)[:, None] * freq[None, :].astype(np.float32)
    angles = angles.astype(np.float64)
    cosine, sine = np.cos(angles), np.sin(angles)
    return (
        np.concatenate([cosine, cosine], axis=1).astype(np.float32),
        np.concatenate([-sine, sine], axis=1).astype(np.float32),
    )


def dot(a, b, ca, cb, **kw):
    return lax.dot_general(a, b, (((ca,), (cb,)), ((), ())), preferred_element_type=F32, **kw)


def rotate(v, c, s):
    return v * c + pltpu.roll(v, H // 2, axis=1) * s


def rotate_back(v, c, s):
    return v * c - pltpu.roll(v, H // 2, axis=1) * s


def kernel(
    x_h, g_h, gain_h, wq_h, wo_h, wkv_h, dwt_h, gup_h, upq_h, upkv_h, odt_h, cos_h, sin_h,
    hid_o, pd_o, ou_o, sm_o,
    xb, gb, nb, wq, wo, wkv, dwt, gup, upq, upk, upv, odt, odb, gain, cosb, sinb, wkv_in, wkv_f, upkv_in, upkv_f,
    ss_own, ss_recv, r_all, ip_own, ip_recv, bo_part, bo_recv, bo_all,
    kvl_part, kvl_pair, kvl_send, kvl_recv, kvl_all,
    a_acc_o, a_acc_s, a_ps_o, a_ps_s, a_pr_o, a_pr_s, a_xs, a_xr, a_ys, a_yr,
    q_acc_o, q_acc_s, q_ps_o, q_ps_s, q_pr_o, q_pr_s, q_xs, q_xr, q_ys, q_yr,
    qrot, dat, attn, dq_own, dq_all, dkacc,
    p1_part, p1_pair, p1_send, p1_recv, dkv_all, dkv_slot, p2_all, back_all, back_slot,
    zpart, rs_sendr, rs_recvr, rs_sendl, rs_recvl, sm_own, sm_recv, ex_own, ex_recv,
    ld, grp_s, grp_r, ring_s, ring_r, kp_s, kp_r, pair_s, pair_r, xm_s, xm_r, yy_s, yy_r,
    dqy_s, dqy_r, dqx_s, dqx_r, dqc_s, dqc_r, rs_s, rs_r, dp_s, dp_r,
):
    d = lax.axis_index("dp")
    f = lax.axis_index("fsdp")
    t = lax.axis_index("tensor")
    c = f // 2
    k = f % 2
    xl = c // 4
    y = c % 4

    def rcopy(src, dst, ss, rs, dev):
        return pltpu.make_async_remote_copy(
            src_ref=src, dst_ref=dst, send_sem=ss, recv_sem=rs, device_id=dev, device_id_type=MESH
        )

    def wait_bytes(ref, sem):
        pltpu.make_async_copy(ref, ref, sem).wait()

    def fdev(i):
        return (d, lax.rem(f + i, NF), t)

    def zdev(i):
        return (d, f, lax.rem(t + i + NT, NT))

    mate = (d, 2 * c + 1 - k, t)
    xmate = (d, 2 * (4 * (1 - xl) + y) + k, t)
    other = (1 - d, f, t)

    def block(slot):
        rel = jnp.where(slot % 2 == 1, (slot + 1) // 2, NT - slot // 2) if not isinstance(slot, int) else (
            (slot + 1) // 2 if slot % 2 == 1 else NT - slot // 2
        )
        return lax.rem(t + rel, NT)

    def block_rows(slot):
        return pl.ds(pl.multiple_of(block(slot) * T, T), T)

    def slot_rows(slot):
        return pl.ds(slot * T, T)

    loads = [
        (g_h, gb.at[slot_rows(0)]),
        (x_h, xb.at[slot_rows(0)]),
        (gain_h, gain),
        (wo_h, wo),
        (wq_h, wq),
        (wkv_h, wkv_in),
        (dwt_h.at[pl.ds(0, 64)], dwt.at[pl.ds(0, 64)]),
        (dwt_h.at[pl.ds(64, 128)], dwt.at[pl.ds(128, 128)]),
        (gup_h, gup.at[pl.ds(0, 64)]),
        (upq_h, upq.at[pl.ds(0, 64)]),
        (upkv_h, upkv_in),
        (odt_h, odt.at[pl.ds(0, 64)]),
        (odt_h, odb.at[pl.ds(64, 64)]),
        (cos_h, cosb),
        (sin_h, sinb),
    ]
    copies = [pltpu.make_async_copy(s, o, ld.at[i]) for i, (s, o) in enumerate(loads)]
    for copy in copies:
        copy.start()

    barrier = pltpu.get_barrier_semaphore()

    @pl.loop(1, NF)
    def _(i):
        pl.semaphore_signal(barrier, inc=1, device_id=fdev(i), device_id_type=MESH)

    @pl.loop(1, NT)
    def _(i):
        pl.semaphore_signal(barrier, inc=1, device_id=zdev(i), device_id_type=MESH)

    pl.semaphore_signal(barrier, inc=1, device_id=other, device_id_type=MESH)

    dwt[pl.ds(64, 64)] = jnp.zeros((64, W), BF16)
    gup[pl.ds(64, 64)] = jnp.zeros((64, W), BF16)
    upq[pl.ds(64, 192)] = jnp.zeros((192, H), BF16)
    upk[pl.ds(0, 128)] = jnp.zeros((128, H), BF16)
    upk[pl.ds(192, 64)] = jnp.zeros((64, H), BF16)
    upv[pl.ds(0, 192)] = jnp.zeros((192, H), BF16)
    odt[pl.ds(64, 64)] = jnp.zeros((64, H), BF16)
    odb[pl.ds(0, 64)] = jnp.zeros((64, H), BF16)
    dkacc[...] = jnp.zeros_like(dkacc)
    copies[0].wait()
    copies[1].wait()
    x_own = xb[slot_rows(0)].astype(F32)
    ones = jnp.ones((8, W), F32)
    squares = dot(ones, x_own * x_own, 1, 1, precision=lax.Precision.HIGHEST)
    ss_own[...] = jnp.concatenate([squares, squares], axis=1)

    pl.semaphore_wait(barrier, NF - 1 + NT - 1 + 1)

    def ring(buf, n):
        def right(s):
            src, dst = (0, 2, 4, 6)[s - 1], (2, 4, 6, 7)[s - 1]
            size = T if s < 4 else T // 2
            return rcopy(
                buf.at[pl.ds(src * T, size)], buf.at[pl.ds(dst * T, size)],
                ring_s.at[n, 0, s - 1], ring_r.at[n, 0, s - 1], zdev(1),
            )

        def left(s):
            src, dst = (0, 1, 3, 5)[s - 1], (1, 3, 5, 7)[s - 1]
            size, off = (T, 0) if s < 4 else (T // 2, T // 2)
            return rcopy(
                buf.at[pl.ds(src * T + off, size)], buf.at[pl.ds(dst * T + off, size)],
                ring_s.at[n, 1, s - 1], ring_r.at[n, 1, s - 1], zdev(-1),
            )

        def start(s):
            right(s).start()
            left(s).start()

        def arrive(s):
            right(s).wait_recv()
            left(s).wait_recv()

        def finish(last=4):
            for s in range(1, last + 1):
                right(s).wait_send()
                left(s).wait_send()

        return start, arrive, finish

    g_start, g_arrive, g_finish = ring(gb, 0)
    x_start, x_arrive, x_finish = ring(xb, 1)

    def column(rows8):
        return rows8.T[:T, 0:1]

    def gain_row():
        return jnp.concatenate([gain[pl.ds(i, 1)] for i in range(8)], axis=1)

    def normalise(slot):
        rows = slot_rows(slot)
        nb[rows] = (xb[rows].astype(F32) * column(r_all[block(slot)]) * gain_row()).astype(BF16)

    def heads(product, chunks, n, bufs):
        acc_o, acc_s, ps_o, ps_s, pr_o, pr_s, xs, xr, ys, yr = bufs

        def rows_of(ch):
            return pl.ds(*chunks[ch])

        def pair_copy(ch, g):
            src, dst = ((ps_o, pr_o), (ps_s, pr_s))[g]
            return rcopy(src.at[:, rows_of(ch)], dst.at[:, rows_of(ch)], pair_s.at[n, ch, g], pair_r.at[n, ch, g], mate)

        def x_copy(ch):
            return rcopy(xs.at[:, rows_of(ch)], xr.at[:, rows_of(ch)], xm_s.at[n, ch], xm_r.at[n, ch], xmate)

        def y_copy(ch, j):
            yj = lax.rem(y + j, 4)
            return rcopy(
                ys.at[yj, rows_of(ch)], yr.at[j - 1, rows_of(ch)], yy_s.at[n, ch, j - 1], yy_r.at[n, ch, j - 1],
                (d, 2 * (4 * xl + yj) + k, t),
            )

        def first(ch, g):
            rows = rows_of(ch)
            acc, ps = ((acc_o, ps_o), (acc_s, ps_s))[g]
            base = 4 * (1 - xl) if g == 0 else 4 * xl

            @pl.loop(0, 4)
            def _(i):
                both = product(rows, base + i)
                acc[i, rows] = jnp.where(k == 0, both[:, :H], both[:, H:])
                ps[i, rows] = jnp.where(k == 0, both[:, H:], both[:, :H]).astype(BF16)

            pair_copy(ch, g).start()

        def second(ch):
            rows = rows_of(ch)
            pair_copy(ch, 0).wait_recv()

            @pl.loop(0, 4)
            def _(i):
                xs[i, rows] = (acc_o[i, rows] + pr_o[i, rows].astype(F32)).astype(BF16)

            x_copy(ch).start()

        def third(ch):
            rows = rows_of(ch)
            pair_copy(ch, 1).wait_recv()
            x_copy(ch).wait_recv()
            for j in range(1, 4):
                yj = lax.rem(y + j, 4)
                ys[yj, rows] = (acc_s[yj, rows] + pr_s[yj, rows].astype(F32) + xr[yj, rows].astype(F32)).astype(BF16)
                y_copy(ch, j).start()

        def total(ch):
            rows = rows_of(ch)
            value = acc_s[y, rows] + pr_s[y, rows].astype(F32) + xr[y, rows].astype(F32)
            for j in range(1, 4):
                y_copy(ch, j).wait_recv()
                value = value + yr[j - 1, rows].astype(F32)
            return value

        def finish():
            for ch in range(len(chunks)):
                pair_copy(ch, 0).wait_send()
                pair_copy(ch, 1).wait_send()
                x_copy(ch).wait_send()
                for j in range(1, 4):
                    y_copy(ch, j).wait_send()

        return first, second, third, total, finish

    def a_product(rows, ci):
        return dot(gb[rows], wo[pl.ds(pl.multiple_of(ci * 256, 256), 256), :], 1, 1)

    def q_product(rows, ci):
        return dot(nb[rows], wq[:, pl.ds(pl.multiple_of(ci * 256, 256), 256)], 1, 0)

    a_chunks = [(0, 64), (64, 128), (192, 128), (320, 192)]
    q_chunks = [(0, 192), (192, 128), (320, 128), (448, 64)]
    a1, a2, a3, a_total, a_finish = heads(
        a_product, a_chunks, 0, (a_acc_o, a_acc_s, a_ps_o, a_ps_s, a_pr_o, a_pr_s, a_xs, a_xr, a_ys, a_yr)
    )
    q1, q2, q3, q_total, q_finish = heads(
        q_product, q_chunks, 1, (q_acc_o, q_acc_s, q_ps_o, q_ps_s, q_pr_o, q_pr_s, q_xs, q_xr, q_ys, q_yr)
    )

    def kvl_copy(ch):
        s0, n = q_chunks[ch][0] // T, q_chunks[ch][1] // T
        return rcopy(
            kvl_part.at[pl.ds(s0, n), 1 - k], kvl_pair.at[pl.ds(s0, n)], kp_s.at[ch], kp_r.at[ch], mate
        )

    def kvl1(ch):
        s0, n = q_chunks[ch][0] // T, q_chunks[ch][1] // T
        rows = pl.ds(*q_chunks[ch])
        kvl_part[pl.ds(s0, n), :, :, pl.ds(0, 256)] = dot(nb[rows], wkv[...], 1, 0).reshape(n, 2, R, 256)
        kvl_part[pl.ds(s0, n), :, :, pl.ds(256, 256)] = dot(nb[rows], dwt[...], 1, 1).reshape(n, 2, R, 256)
        kvl_copy(ch).start()

    def to_chip(send, recv, s, n):
        @pl.when(s != c)
        def _():
            rcopy(send.at[s], recv.at[c], grp_s.at[n], grp_r.at[n], (d, 2 * s + k, t)).start()

    def kvl2(ch):
        s0, n = q_chunks[ch][0] // T, q_chunks[ch][1] // T
        kvl_copy(ch).wait_recv()
        for s in range(s0, s0 + n):
            kvl_send[s] = kvl_part[s, k] + kvl_pair[s]
            to_chip(kvl_send, kvl_recv, s, 5)

    def chip_total(own, recv):
        def add(i, total):
            return total + recv[lax.rem(c + i, NC)].astype(F32)

        return lax.fori_loop(1, NC, add, own)

    def gather_chips(buf, z, n):
        ref = buf.at[z, k]

        @pl.loop(1, NC)
        def _(i):
            rcopy(ref, ref, grp_s.at[n], grp_r.at[n], (d, 2 * lax.rem(c + i, NC) + k, t)).start()

    def gather_mate(buf, n):
        return rcopy(buf.at[:, k], buf.at[:, k], grp_s.at[n], grp_r.at[n], mate)

    def seven(buf):
        return buf.at[pl.ds(0, NC - 1), 0]

    def total_f(own, recv):
        def add(i, total):
            return total + recv[i].astype(F32)

        return lax.fori_loop(0, NF - 1, add, own.astype(F32))

    g_start(1)
    x_start(1)

    @pl.loop(1, NF)
    def _(i):
        rcopy(ss_own, ss_recv.at[i - 1], grp_s.at[0], grp_r.at[0], fdev(i)).start()

    copies[3].wait()
    a1(0, 0)
    a1(0, 1)
    a2(0)
    wait_bytes(ss_recv, grp_r.at[0])
    squares = total_f(ss_own[...], ss_recv)
    r_all[t] = lax.rsqrt(squares / (W * NF) + eps)

    @pl.loop(1, NT)
    def _(i):
        rcopy(r_all.at[t], r_all.at[t], grp_s.at[1], grp_r.at[1], zdev(i)).start()

    g_arrive(1)
    g_start(2)
    a1(1, 0)
    x_arrive(1)
    x_start(2)
    a1(1, 1)
    a2(1)
    a3(0)
    for i in (2, 4, 5, 6, 7, 8, 9, 10):
        copies[i].wait()
    wkv_f[...] = wkv_in[...].astype(F32)
    wkv[:, pl.ds(0, H)] = wkv_f[pl.ds(0, W, stride=2)].astype(BF16)
    wkv[:, pl.ds(H, H)] = wkv_f[pl.ds(1, W, stride=2)].astype(BF16)
    upkv_f[...] = upkv_in[...].astype(F32)
    upk[pl.ds(128, 64)] = upkv_f[pl.ds(0, 64, stride=2)].astype(BF16)
    upv[pl.ds(192, 64)] = upkv_f[pl.ds(1, 64, stride=2)].astype(BF16)
    g_arrive(2)
    g_start(3)
    wait_bytes(r_all.at[pl.ds(0, NT - 1)], grp_r.at[1])
    for slot in range(3):
        normalise(slot)
    kvl1(0)
    x_arrive(2)
    x_start(3)
    q1(0, 0)
    q1(0, 1)
    kvl2(0)
    q2(0)
    g_arrive(3)
    g_start(4)
    normalise(3)
    normalise(4)
    kvl1(1)
    a1(2, 0)
    a3(1)
    a1(2, 1)
    x_arrive(3)
    x_start(4)
    kvl2(1)
    q1(1, 0)
    a2(2)
    q3(0)
    q1(1, 1)
    q2(1)
    normalise(5)
    normalise(6)
    kvl1(2)
    q1(2, 0)
    g_arrive(4)
    bo_part[...] = dot(gb[...], gup[...], 1, 1).astype(BF16)

    @pl.loop(1, NF)
    def _(i):
        fi = lax.rem(f + i, NF)
        rcopy(
            bo_part.at[pl.ds(pl.multiple_of(fi * R, R), R)], bo_recv.at[i - 1], grp_s.at[2], grp_r.at[2], (d, fi, t)
        ).start()

    kvl2(2)
    x_arrive(4)
    normalise(7)
    kvl1(3)
    q1(2, 1)
    kvl2(3)
    q1(3, 0)
    q2(2)
    q1(3, 1)
    q2(3)
    q3(1)
    a3(2)
    z_own = block(c)
    own_slots = pl.ds(pl.multiple_of(f * R, R), R)
    own_rows = pl.ds(pl.multiple_of(z_own * T + k * R, R), R)
    for i in range(11, 15):
        copies[i].wait()
    wait_bytes(kvl_recv.at[pl.ds(0, NC - 1)], grp_r.at[5])
    total = chip_total(kvl_send[c], kvl_recv)
    low = total[:, 256:].astype(BF16)
    keys = total[:, :H] + adapter_scale * dot(low, upk[...], 1, 0)
    values = total[:, H:256] + adapter_scale * dot(low, upv[...], 1, 0)
    keys = rotate(keys, cosb[own_rows], sinb[own_rows])
    kvl_all[z_own, k, :, pl.ds(0, H)] = keys.astype(BF16)
    kvl_all[z_own, k, :, pl.ds(H, H)] = values.astype(BF16)
    kvl_all[z_own, k, :, pl.ds(256, 256)] = low
    gather_chips(kvl_all, z_own, 6)
    wait_bytes(bo_recv, grp_r.at[2])
    bo_all[own_rows] = total_f(bo_part[own_slots], bo_recv).astype(BF16)
    bo_ref = bo_all.at[own_rows]

    @pl.loop(1, NF)
    def _(i):
        rcopy(bo_ref, bo_ref, grp_s.at[3], grp_r.at[3], fdev(i)).start()

    a1(3, 0)
    q3(2)
    a2(3)
    q3(3)
    a1(3, 1)
    a3(3)
    wait_bytes(seven(kvl_all), grp_r.at[6])
    gather_mate(kvl_all, 7).start()

    def a_store(ch):
        value = a_total(ch)
        r0, size = a_chunks[ch]
        for s in range(r0 // T, (r0 + size) // T):
            part = value[s * T - r0 : (s + 1) * T - r0]
            rows = block_rows(s)
            dat[rows] = (part + adapter_scale * dot(bo_all[rows], odt[...], 1, 0)).astype(BF16)

    wait_bytes(bo_all.at[pl.ds(0, (NF - 1) * R)], grp_r.at[3])
    for ch in range(3):
        a_store(ch)
    gather_mate(kvl_all, 7).wait_recv()
    for ch, (r0, size) in enumerate(q_chunks):
        value = q_total(ch)
        for s in range(r0 // T, (r0 + size) // T):
            part = value[s * T - r0 : (s + 1) * T - r0]
            rows = block_rows(s)
            low = kvl_all[block(s), :, :, pl.ds(256, 256)].reshape(T, 256)
            query = part + adapter_scale * dot(low, upq[...], 1, 0)
            qrot[rows] = rotate(query, cosb[rows], sinb[rows]).astype(BF16)
    a_store(3)

    scale = 1.0 / math.sqrt(H)
    for i in range(4):
        rows = pl.ds(i * 128, 128)
        n = (i + 1) * 128
        seen = pl.ds(0, n)
        krot = kvl_all[pl.ds(0, n // T), :, :, pl.ds(0, H)].reshape(n, H)
        vals = kvl_all[pl.ds(0, n // T), :, :, pl.ds(H, H)].reshape(n, H)
        qi = qrot[rows]
        da = dat[rows]
        scores = dot(qi, krot, 1, 1) * scale
        causal = lax.broadcasted_iota(jnp.int32, (128, n), 0) + i * 128 >= lax.broadcasted_iota(
            jnp.int32, (128, n), 1
        )
        scores = jnp.where(causal, scores, -1e30)
        e = jnp.exp(scores - jnp.max(scores, axis=1, keepdims=True))
        probs = e / jnp.sum(e, axis=1, keepdims=True)
        probs_b = probs.astype(BF16)
        attn[rows] = dot(probs_b, vals, 1, 0).astype(BF16)
        dprobs = dot(da, vals, 1, 1)
        delta = jnp.sum(probs * dprobs, axis=1, keepdims=True)
        dscore = (probs * (dprobs - delta) * scale).astype(BF16)
        dquery = dot(dscore, krot, 1, 0)
        dq_own[rows] = rotate_back(dquery, cosb[rows], sinb[rows]).astype(BF16)
        dkacc[seen, pl.ds(0, H)] += dot(dscore, qi, 0, 0)
        dkacc[seen, pl.ds(H, H)] += dot(probs_b, da, 0, 0)

    z_chunks = [(448, 64), (320, 128), (192, 128), (0, 192)]

    def dqy_copy(ch, j):
        ref = dq_all.at[xl, y, k, pl.ds(*z_chunks[ch])]
        return rcopy(
            ref, ref, dqy_s.at[ch, j - 1], dqy_r.at[ch, j - 1], (d, 2 * (4 * xl + lax.rem(y + j, 4)) + k, t)
        )

    def dqx_copy(ch):
        ref = dq_all.at[xl, :, k, pl.ds(*z_chunks[ch])]
        return rcopy(ref, ref, dqx_s.at[ch], dqx_r.at[ch], xmate)

    def dqc_copy(ch, g):
        ref = dq_all.at[xl if g == 0 else 1 - xl, :, k, pl.ds(*z_chunks[ch])]
        return rcopy(ref, ref, dqc_s.at[ch, g], dqc_r.at[ch, g], mate)

    def dq_send(ch):
        r0, size = z_chunks[ch]
        for s in range(r0 // T, (r0 + size) // T):
            dq_all[xl, y, k, slot_rows(s)] = dq_own[block_rows(s)]
        for j in range(1, 4):
            dqy_copy(ch, j).start()

    def dq_forward_x(ch):
        for j in range(1, 4):
            dqy_copy(ch, j).wait_recv()
        dqx_copy(ch).start()
        dqc_copy(ch, 0).start()

    def dq_forward_core(ch):
        dqx_copy(ch).wait_recv()
        dqc_copy(ch, 1).start()

    dq_send(0)
    p1_part[:, :, :, pl.ds(0, 256)] = dkacc[...].reshape(NC, 2, R, 256)
    p1_part[:, :, :, pl.ds(256, H)] = (
        dot(dq_own[...], upq[pl.ds(0, H)], 1, 1) + dot(attn[...], odb[...], 1, 1)
    ).reshape(NC, 2, R, H)
    p1_copy = rcopy(p1_part.at[:, 1 - k], p1_pair, grp_s.at[8], grp_r.at[8], mate)
    p1_copy.start()
    sm_own[pl.ds(192, 64)] = dot(bo_all[...], attn[...], 0, 0)[:64]
    p1_copy.wait_recv()
    for s in range(NC):
        p1_send[s] = (p1_part[s, k] + p1_pair[s]).astype(BF16)
        to_chip(p1_send, p1_recv, s, 9)
    dq_send(1)
    all_low = kvl_all[:, :, :, pl.ds(256, 256)].reshape(L, 256)
    sm_own[pl.ds(0, 64)] = dot(all_low, dq_own[...], 0, 0)[:64]
    dq_forward_x(0)
    wait_bytes(p1_recv.at[pl.ds(0, NC - 1)], grp_r.at[9])
    total = chip_total(p1_part[c, k] + p1_pair[c], p1_recv)
    piece = pl.ds(pl.multiple_of(f * R, R), R)
    dkey = rotate_back(total[:, :H], cosb[piece], sinb[piece]).astype(BF16)
    dval = total[:, H:256].astype(BF16)
    dkv_all[c, k, :, pl.ds(0, H)] = dkey
    dkv_all[c, k, :, pl.ds(H, H)] = dval
    gather_chips(dkv_all, c, 10)
    p2_all[t, :, pl.ds(0, H)] = total[:, 256:].astype(BF16)
    p2_all[t, :, pl.ds(H, H)] = (
        dot(dkey, upk[pl.ds(H, H)], 1, 1) + dot(dval, upv[pl.ds(H, H)], 1, 1)
    ).astype(BF16)

    @pl.loop(1, NT)
    def _(i):
        rcopy(p2_all.at[t], p2_all.at[t], grp_s.at[12], grp_r.at[12], zdev(i)).start()

    dq_forward_core(0)
    dq_forward_x(1)
    dq_send(2)
    dq_send(3)
    wait_bytes(seven(dkv_all), grp_r.at[10])
    gather_mate(dkv_all, 11).start()
    wait_bytes(p2_all.at[pl.ds(0, NT - 1)], grp_r.at[12])
    total = p2_all[0].astype(F32)
    for i in range(1, NT):
        total = total + p2_all[i].astype(F32)
    back_all[c, k] = total.astype(BF16)
    gather_chips(back_all, c, 13)
    gather_mate(dkv_all, 11).wait_recv()
    for s in range(NT):
        dkv_slot[slot_rows(s)] = dkv_all[block(s)].reshape(T, 256)

    def slots_of(j, way):
        far = ([7, 5, 3, 1], [7, 6, 4, 2])[way]
        return far if j % 2 == way else far[1:]

    def rs_copy(j, way, s):
        send, recv = ((rs_sendr, rs_recvr), (rs_sendl, rs_recvl))[way]
        return rcopy(
            send.at[j, s], recv.at[j, s], rs_s.at[way, j, s], rs_r.at[way, j, s], zdev(1 - 2 * way)
        )

    def rs_step(j, way, s):
        value = zpart[j, slot_rows(slots_of(j, way)[s])]
        send, recv = ((rs_sendr, rs_recvr), (rs_sendl, rs_recvl))[way]
        if s > 0:
            rs_copy(j, way, s - 1).wait_recv()
            value = value + recv[j, s - 1].astype(F32)
        send[j, s] = value.astype(BF16)
        rs_copy(j, way, s).start()

    for ch in range(4):
        rows = pl.ds(*z_chunks[ch])
        if ch == 1:
            dq_forward_core(1)
            dq_forward_x(2)
        if ch == 2:
            dq_forward_core(2)
            dq_forward_x(3)
        if ch == 3:
            dq_forward_core(3)
        dqc_copy(ch, 0).wait_recv()
        dqc_copy(ch, 1).wait_recv()
        dq = jnp.concatenate([dq_all[i // 8, i // 2 % 4, i % 2, rows] for i in range(NF)], axis=1)
        for j in range(4):
            wide = pl.ds(j * 256, 256)
            zpart[j, rows] = dot(dq, wq[wide, :], 1, 1) + dot(dkv_slot[rows], wkv[wide, :], 1, 1)
            for way in range(2):
                s = ch if j % 2 == way else ch - 1
                if s >= 0:
                    rs_step(j, way, s)
        if ch == 1:
            wait_bytes(seven(back_all), grp_r.at[13])
            gather_mate(back_all, 14).start()

    gather_mate(back_all, 14).wait_recv()
    for s in range(NT):
        back_slot[slot_rows(s)] = back_all[block(s)].reshape(T, 256)
    halves = []
    for i in range(2):
        rows = pl.ds(i * 128, 128)
        ex_own[rows] = dot(back_slot[:, rows], nb[...], 0, 0).astype(BF16)
        if i == 0:
            ex_own[pl.ds(64, 64)] = dot(back_slot[:, rows], gb[...], 0, 0)[64:].astype(BF16)
        halves.append(rcopy(ex_own.at[rows], ex_recv.at[rows], dp_s.at[1 + i], dp_r.at[1 + i], other))
        halves[i].start()
    kv_up = dot(all_low, dkv_all[...].reshape(L, 256), 0, 0)
    sm_own[pl.ds(64, 64)] = kv_up[128:192, :H]
    sm_own[pl.ds(128, 64)] = kv_up[192:, H:]
    small = rcopy(sm_own, sm_recv, dp_s.at[0], dp_r.at[0], other)
    small.start()

    inverse = column(r_all[t])
    xhat = x_own * inverse
    dhat = []
    for j in range(4):
        wide = pl.ds(j * 256, 256)
        value = zpart[j, slot_rows(0)] + adapter_scale * dot(back_slot[slot_rows(0)], dwt[:, wide], 1, 0)
        for way, recv in enumerate((rs_recvr, rs_recvl)):
            last = len(slots_of(j, way)) - 1
            rs_copy(j, way, last).wait_recv()
            value = value + recv[j, last].astype(F32)
        dhat.append(value)
    dhat = jnp.concatenate(dhat, axis=1) * gain_row()
    inner = dot(ones, dhat * xhat, 1, 1, precision=lax.Precision.HIGHEST)
    ip_own[...] = jnp.concatenate([inner, inner], axis=1)

    @pl.loop(1, NF)
    def _(i):
        rcopy(ip_own, ip_recv.at[i - 1], grp_s.at[15], grp_r.at[15], fdev(i)).start()

    small.wait_recv()
    both = adapter_scale * (sm_own[...] + sm_recv[...])
    sm_o[pl.ds(0, 64)] = both[:64]
    sm_o[pl.ds(64, 64, stride=2)] = both[64:128]
    sm_o[pl.ds(65, 64, stride=2)] = both[128:192]
    sm_o[pl.ds(192, 64)] = both[192:]
    wait_bytes(ip_recv, grp_r.at[15])
    inner = total_f(ip_own[...], ip_recv) / (W * NF)
    hid_o[...] = gb[slot_rows(0)].astype(F32) + inverse * (dhat - xhat * column(inner))
    halves[0].wait_recv()

    def added(i, n):
        return adapter_scale * (ex_own[pl.ds(i, n)].astype(F32) + ex_recv[pl.ds(i, n)].astype(F32))

    pd_o[pl.ds(0, 64)] = added(0, 64)
    ou_o[...] = added(64, 64)
    halves[1].wait_recv()
    pd_o[pl.ds(64, 128)] = added(128, 128)

    g_finish()
    x_finish()
    a_finish()
    q_finish()
    for ch in range(4):
        kvl_copy(ch).wait_send()
        dqx_copy(ch).wait_send()
        dqc_copy(ch, 0).wait_send()
        dqc_copy(ch, 1).wait_send()
        for j in range(1, 4):
            dqy_copy(ch, j).wait_send()
    for j in range(4):
        for way in range(2):
            for s in range(len(slots_of(j, way))):
                rs_copy(j, way, s).wait_send()
    p1_copy.wait_send()
    small.wait_send()
    for half in halves:
        half.wait_send()
    gather_mate(kvl_all, 7).wait_send()
    gather_mate(dkv_all, 11).wait_send()
    gather_mate(back_all, 14).wait_send()
    sent = {
        0: ss_recv, 1: r_all.at[pl.ds(0, NT - 1)], 2: bo_recv, 3: bo_all.at[pl.ds(0, (NF - 1) * R)],
        5: kvl_recv.at[pl.ds(0, NC - 1)], 6: seven(kvl_all), 9: p1_recv.at[pl.ds(0, NC - 1)], 10: seven(dkv_all),
        12: p2_all.at[pl.ds(0, NT - 1)], 13: seven(back_all), 15: ip_recv,
    }
    for n, ref in sent.items():
        wait_bytes(ref, grp_s.at[n])


def hand_over(hid, pd, ou, sm, hid_o, pd_o, ou_o, qu_o, ku_o, od_o):
    hid_o[...] = hid[...]
    pd_o[...] = pd[...]
    ou_o[...] = ou[...]
    qu_o[...] = sm[pl.ds(0, 64)]
    ku_o[...] = sm[pl.ds(64, 128)]
    od_o[...] = sm[pl.ds(192, 64)]


def local(
    residual_input,
    block_output_gradient,
    norm_gain_vector,
    query_matrix,
    keyvalue_matrix,
    output_matrix,
    adapter_projection_down,
    adapter_query_up,
    adapter_keyvalue_up,
    adapter_output_down,
    adapter_output_up,
):
    cosine, sine = rope_tables()
    vm = pltpu.VMEM
    dma = pltpu.SemaphoreType.DMA
    quarter = [vm((4, L, H), BF16)] * 7 + [vm((3, L, H), BF16)]
    heads = [vm((4, L, H), F32)] * 2 + quarter
    scratch = [
        vm((L, W), BF16), vm((L, W), BF16), vm((L, W), BF16),
        vm((W, 2048), BF16), vm((2048, W), BF16), vm((W, 256), BF16), vm((256, W), BF16), vm((128, W), BF16),
        vm((256, H), BF16), vm((256, H), BF16), vm((256, H), BF16), vm((128, H), BF16), vm((128, H), BF16),
        vm((8, H), F32), vm((L, H), F32), vm((L, H), F32),
        vm((2 * W, H), BF16), vm((2 * W, H), F32), vm((128, H), BF16), vm((128, H), F32),
        vm((8, H), F32), vm((NF - 1, 8, H), F32), vm((NT, 8, H), F32), vm((8, H), F32), vm((NF - 1, 8, H), F32),
        vm((L, H), BF16), vm((NF - 1, R, H), BF16), vm((L, H), BF16),
        vm((NC, 2, R, 512), F32), vm((NC, R, 512), F32), vm((NC, R, 512), F32), vm((NC, R, 512), F32),
        vm((NC, 2, R, 512), BF16),
        *heads, *heads,
        vm((L, H), BF16), vm((L, H), BF16), vm((L, H), BF16), vm((L, H), BF16), vm((2, 4, 2, L, H), BF16),
        vm((L, 256), F32),
        vm((NC, 2, R, 384), F32), vm((NC, R, 384), F32), vm((NC, R, 384), BF16), vm((NC, R, 384), BF16),
        vm((NC, 2, R, 256), BF16), vm((L, 256), BF16), vm((NT, R, 256), BF16),
        vm((NC, 2, R, 256), BF16), vm((L, 256), BF16),
        vm((4, L, 256), F32),
        vm((4, 4, T, 256), BF16), vm((4, 4, T, 256), BF16), vm((4, 4, T, 256), BF16), vm((4, 4, T, 256), BF16),
        vm((256, H), F32), vm((256, H), F32), vm((256, W), BF16), vm((256, W), BF16),
        dma((16,)), dma((16,)), dma((16,)), dma((2, 2, 4)), dma((2, 2, 4)), dma((4,)), dma((4,)),
        dma((2, 4, 2)), dma((2, 4, 2)), dma((2, 4)), dma((2, 4)), dma((2, 4, 3)), dma((2, 4, 3)),
        dma((4, 3)), dma((4, 3)), dma((4,)), dma((4,)), dma((4, 2)), dma((4, 2)),
        dma((2, 4, 4)), dma((2, 4, 4)), dma((3,)), dma((3,)),
    ]
    hidden, down, up, small = pl.pallas_call(
        kernel,
        out_shape=(
            jax.ShapeDtypeStruct((T, W), F32),
            jax.ShapeDtypeStruct((192, W), F32),
            jax.ShapeDtypeStruct((64, W), F32),
            jax.ShapeDtypeStruct((256, H), F32),
        ),
        in_specs=[pl.BlockSpec(memory_space=pl.ANY)] * 13,
        out_specs=(pl.BlockSpec(memory_space=pltpu.VMEM),) * 4,
        scratch_shapes=scratch,
        compiler_params=pltpu.CompilerParams(
            collective_id=0, has_side_effects=True, vmem_limit_bytes=60 * 2**20
        ),
        name="adapter_backward",
    )(
        residual_input[0],
        block_output_gradient[0],
        norm_gain_vector.reshape(8, H),
        query_matrix[:, 0, :],
        output_matrix[0],
        keyvalue_matrix.reshape(2 * W, H),
        adapter_projection_down.T,
        adapter_output_up,
        adapter_query_up[:, 0, :],
        adapter_keyvalue_up.reshape(128, H),
        adapter_output_down[0].T,
        jnp.asarray(cosine),
        jnp.asarray(sine),
    )
    hidden, down, up, query_up, keyvalue_up, output_down = pl.pallas_call(
        hand_over,
        out_shape=(
            jax.ShapeDtypeStruct((T, W), F32),
            jax.ShapeDtypeStruct((192, W), F32),
            jax.ShapeDtypeStruct((64, W), F32),
            jax.ShapeDtypeStruct((64, H), F32),
            jax.ShapeDtypeStruct((128, H), F32),
            jax.ShapeDtypeStruct((64, H), F32),
        ),
        in_specs=[pl.BlockSpec(memory_space=pltpu.VMEM)] * 4,
        out_specs=(pl.BlockSpec(memory_space=pltpu.VMEM),) * 6,
        name="hand_over",
    )(hidden, down, up, small)
    return (
        hidden[None],
        down.T,
        query_up[:, None, :],
        keyvalue_up.reshape(64, 2, H),
        output_down.T[None],
        up,
    )


def solution(mesh):
    in_specs = (
        P("dp", "tensor", "fsdp"),
        P("dp", "tensor", "fsdp"),
        P("fsdp"),
        P("fsdp", "tensor", None),
        P("fsdp", None, "tensor"),
        P("tensor", None, "fsdp"),
        P("fsdp", None),
        P(None, "tensor", "fsdp"),
        P(None, None, "tensor"),
        P("tensor", "fsdp", None),
        P(None, "fsdp"),
    )
    out_specs = (
        P("dp", "tensor", "fsdp"),
        P("fsdp", None),
        P(None, "tensor", "fsdp"),
        P(None, None, "tensor"),
        P("tensor", "fsdp", None),
        P(None, "fsdp"),
    )
    return jax.shard_map(local, mesh=mesh, in_specs=in_specs, out_specs=out_specs, check_vma=False)
```

```python
import math

import jax
import jax.numpy as jnp
import numpy as np
from jax import lax
from jax.experimental import pallas as pl
from jax.experimental.pallas import tpu as pltpu
from jax.sharding import PartitionSpec as P

eps = 1e-05
adapter_scale = 2.0
theta = 500000.0
MESH = pl.DeviceIdType.MESH
F32 = jnp.float32
BF16 = jnp.bfloat16

NF = 16
NC = 8
NT = 8
L = 512
T = 64
W = 1024
H = 128
R = 32


def rope_tables():
    half = H // 2
    freq = np.float32(theta) ** (-(np.arange(half, dtype=np.float32) * np.float32(2.0)) / np.float32(H))
    angles = np.arange(L, dtype=np.float32)[:, None] * freq[None, :].astype(np.float32)
    angles = angles.astype(np.float64)
    cosine, sine = np.cos(angles), np.sin(angles)
    return (
        np.concatenate([cosine, cosine], axis=1).astype(np.float32),
        np.concatenate([-sine, sine], axis=1).astype(np.float32),
    )


def dot(a, b, ca, cb, **kw):
    return lax.dot_general(a, b, (((ca,), (cb,)), ((), ())), preferred_element_type=F32, **kw)


def rotate(v, c, s):
    return v * c + pltpu.roll(v, H // 2, axis=1) * s


def rotate_back(v, c, s):
    return v * c - pltpu.roll(v, H // 2, axis=1) * s


def kernel(
    x_h, g_h, gain_h, wq_h, wo_h, wkv_h, dwt_h, gup_h, upq_h, upkv_h, odt_h, cos_h, sin_h,
    hid_o, pd_o, ou_o, sm_o,
    xb, gb, nb, wq, wo, wkv, dwt, gup, upq, upk, upv, odt, odb, gain, cosb, sinb, wkv_in, wkv_f, upkv_in, upkv_f,
    ss_own, ss_recv, r_all, ip_own, ip_recv, bo_part, bo_recv, bo_all,
    kvl_part, kvl_pair, kvl_send, kvl_recv, kvl_all,
    a_acc_o, a_acc_s, a_ps_o, a_ps_s, a_pr_o, a_pr_s, a_xs, a_xr, a_ys, a_yr,
    q_acc_o, q_acc_s, q_ps_o, q_ps_s, q_pr_o, q_pr_s, q_xs, q_xr, q_ys, q_yr,
    qrot, dat, attn, dq_own, dq_all, dkacc,
    p1_part, p1_pair, p1_send, p1_recv, dkv_all, dkv_slot, p2_all, back_all, back_slot,
    zpart, rs_sendr, rs_recvr, rs_sendl, rs_recvl, sm_own, sm_recv, ex_own, ex_recv,
    ld, grp_s, grp_r, ring_s, ring_r, kp_s, kp_r, pair_s, pair_r, xm_s, xm_r, yy_s, yy_r,
    dqy_s, dqy_r, dqx_s, dqx_r, dqc_s, dqc_r, rs_s, rs_r, dp_s, dp_r,
):
    d = lax.axis_index("dp")
    f = lax.axis_index("fsdp")
    t = lax.axis_index("tensor")
    c = f // 2
    k = f % 2
    xl = c // 4
    y = c % 4

    def rcopy(src, dst, ss, rs, dev):
        return pltpu.make_async_remote_copy(
            src_ref=src, dst_ref=dst, send_sem=ss, recv_sem=rs, device_id=dev, device_id_type=MESH
        )

    def wait_bytes(ref, sem):
        pltpu.make_async_copy(ref, ref, sem).wait()

    def fdev(i):
        return (d, lax.rem(f + i, NF), t)

    def zdev(i):
        return (d, f, lax.rem(t + i + NT, NT))

    mate = (d, 2 * c + 1 - k, t)
    xmate = (d, 2 * (4 * (1 - xl) + y) + k, t)
    other = (1 - d, f, t)

    def block(slot):
        rel = jnp.where(slot % 2 == 1, (slot + 1) // 2, NT - slot // 2) if not isinstance(slot, int) else (
            (slot + 1) // 2 if slot % 2 == 1 else NT - slot // 2
        )
        return lax.rem(t + rel, NT)

    def block_rows(slot):
        return pl.ds(pl.multiple_of(block(slot) * T, T), T)

    def slot_rows(slot):
        return pl.ds(slot * T, T)

    loads = [
        (g_h, gb.at[slot_rows(0)]),
        (x_h, xb.at[slot_rows(0)]),
        (gain_h, gain),
        (wo_h, wo),
        (wq_h, wq),
        (wkv_h, wkv_in),
        (dwt_h.at[pl.ds(0, 64)], dwt.at[pl.ds(0, 64)]),
        (dwt_h.at[pl.ds(64, 128)], dwt.at[pl.ds(128, 128)]),
        (gup_h, gup.at[pl.ds(0, 64)]),
        (upq_h, upq.at[pl.ds(0, 64)]),
        (upkv_h, upkv_in),
        (odt_h, odt.at[pl.ds(0, 64)]),
        (odt_h, odb.at[pl.ds(64, 64)]),
        (cos_h, cosb),
        (sin_h, sinb),
    ]
    copies = [pltpu.make_async_copy(s, o, ld.at[i]) for i, (s, o) in enumerate(loads)]
    for copy in copies:
        copy.start()

    barrier = pltpu.get_barrier_semaphore()

    @pl.loop(1, NF)
    def _(i):
        pl.semaphore_signal(barrier, inc=1, device_id=fdev(i), device_id_type=MESH)

    @pl.loop(1, NT)
    def _(i):
        pl.semaphore_signal(barrier, inc=1, device_id=zdev(i), device_id_type=MESH)

    pl.semaphore_signal(barrier, inc=1, device_id=other, device_id_type=MESH)

    dwt[pl.ds(64, 64)] = jnp.zeros((64, W), BF16)
    gup[pl.ds(64, 64)] = jnp.zeros((64, W), BF16)
    upq[pl.ds(64, 192)] = jnp.zeros((192, H), BF16)
    upk[pl.ds(0, 128)] = jnp.zeros((128, H), BF16)
    upk[pl.ds(192, 64)] = jnp.zeros((64, H), BF16)
    upv[pl.ds(0, 192)] = jnp.zeros((192, H), BF16)
    odt[pl.ds(64, 64)] = jnp.zeros((64, H), BF16)
    odb[pl.ds(0, 64)] = jnp.zeros((64, H), BF16)
    dkacc[...] = jnp.zeros_like(dkacc)
    copies[0].wait()
    copies[1].wait()
    x_own = xb[slot_rows(0)].astype(F32)
    ones = jnp.ones((8, W), F32)
    squares = dot(ones, x_own * x_own, 1, 1, precision=lax.Precision.HIGHEST)
    ss_own[...] = jnp.concatenate([squares, squares], axis=1)

    copies[5].wait()
    copies[10].wait()
    wkv_f[...] = wkv_in[...].astype(F32)
    wkv[:, pl.ds(0, H)] = wkv_f[pl.ds(0, W, stride=2)].astype(BF16)
    wkv[:, pl.ds(H, H)] = wkv_f[pl.ds(1, W, stride=2)].astype(BF16)
    upkv_f[...] = upkv_in[...].astype(F32)
    upk[pl.ds(128, 64)] = upkv_f[pl.ds(0, 64, stride=2)].astype(BF16)
    upv[pl.ds(192, 64)] = upkv_f[pl.ds(1, 64, stride=2)].astype(BF16)
    pl.semaphore_wait(barrier, NF - 1 + NT - 1 + 1)

    def ring(buf, n):
        def right(s):
            src, dst = (0, 2, 4, 6)[s - 1], (2, 4, 6, 7)[s - 1]
            size = T if s < 4 else T // 2
            return rcopy(
                buf.at[pl.ds(src * T, size)], buf.at[pl.ds(dst * T, size)],
                ring_s.at[n, 0, s - 1], ring_r.at[n, 0, s - 1], zdev(1),
            )

        def left(s):
            src, dst = (0, 1, 3, 5)[s - 1], (1, 3, 5, 7)[s - 1]
            size, off = (T, 0) if s < 4 else (T // 2, T // 2)
            return rcopy(
                buf.at[pl.ds(src * T + off, size)], buf.at[pl.ds(dst * T + off, size)],
                ring_s.at[n, 1, s - 1], ring_r.at[n, 1, s - 1], zdev(-1),
            )

        def start(s):
            right(s).start()
            left(s).start()

        def arrive(s):
            right(s).wait_recv()
            left(s).wait_recv()

        def finish(last=4):
            for s in range(1, last + 1):
                right(s).wait_send()
                left(s).wait_send()

        return start, arrive, finish

    g_start, g_arrive, g_finish = ring(gb, 0)
    x_start, x_arrive, x_finish = ring(xb, 1)

    def column(rows8):
        return rows8.T[:T, 0:1]

    def gain_row():
        return jnp.concatenate([gain[pl.ds(i, 1)] for i in range(8)], axis=1)

    def normalise(slot):
        rows = slot_rows(slot)
        nb[rows] = (xb[rows].astype(F32) * column(r_all[block(slot)]) * gain_row()).astype(BF16)

    def heads(product, chunks, n, bufs):
        acc_o, acc_s, ps_o, ps_s, pr_o, pr_s, xs, xr, ys, yr = bufs

        def rows_of(ch):
            return pl.ds(*chunks[ch])

        def pair_copy(ch, g):
            src, dst = ((ps_o, pr_o), (ps_s, pr_s))[g]
            return rcopy(src.at[:, rows_of(ch)], dst.at[:, rows_of(ch)], pair_s.at[n, ch, g], pair_r.at[n, ch, g], mate)

        def x_copy(ch):
            return rcopy(xs.at[:, rows_of(ch)], xr.at[:, rows_of(ch)], xm_s.at[n, ch], xm_r.at[n, ch], xmate)

        def y_copy(ch, j):
            yj = lax.rem(y + j, 4)
            return rcopy(
                ys.at[yj, rows_of(ch)], yr.at[j - 1, rows_of(ch)], yy_s.at[n, ch, j - 1], yy_r.at[n, ch, j - 1],
                (d, 2 * (4 * xl + yj) + k, t),
            )

        def first(ch, g):
            rows = rows_of(ch)
            acc, ps = ((acc_o, ps_o), (acc_s, ps_s))[g]
            base = 4 * (1 - xl) if g == 0 else 4 * xl

            @pl.loop(0, 4)
            def _(i):
                both = product(rows, base + i)
                acc[i, rows] = jnp.where(k == 0, both[:, :H], both[:, H:])
                ps[i, rows] = jnp.where(k == 0, both[:, H:], both[:, :H]).astype(BF16)

            pair_copy(ch, g).start()

        def second(ch):
            rows = rows_of(ch)
            pair_copy(ch, 0).wait_recv()

            @pl.loop(0, 4)
            def _(i):
                xs[i, rows] = (acc_o[i, rows] + pr_o[i, rows].astype(F32)).astype(BF16)

            x_copy(ch).start()

        def third(ch):
            rows = rows_of(ch)
            pair_copy(ch, 1).wait_recv()
            x_copy(ch).wait_recv()
            for j in range(1, 4):
                yj = lax.rem(y + j, 4)
                ys[yj, rows] = (acc_s[yj, rows] + pr_s[yj, rows].astype(F32) + xr[yj, rows].astype(F32)).astype(BF16)
                y_copy(ch, j).start()

        def total(ch):
            rows = rows_of(ch)
            value = acc_s[y, rows] + pr_s[y, rows].astype(F32) + xr[y, rows].astype(F32)
            for j in range(1, 4):
                y_copy(ch, j).wait_recv()
                value = value + yr[j - 1, rows].astype(F32)
            return value

        def finish():
            for ch in range(len(chunks)):
                pair_copy(ch, 0).wait_send()
                pair_copy(ch, 1).wait_send()
                x_copy(ch).wait_send()
                for j in range(1, 4):
                    y_copy(ch, j).wait_send()

        return first, second, third, total, finish

    def a_product(rows, ci):
        return dot(gb[rows], wo[pl.ds(pl.multiple_of(ci * 256, 256), 256), :], 1, 1)

    def q_product(rows, ci):
        return dot(nb[rows], wq[:, pl.ds(pl.multiple_of(ci * 256, 256), 256)], 1, 0)

    a_chunks = [(0, 64), (64, 128), (192, 128), (320, 128), (448, 64)]
    q_chunks = [(0, 192), (192, 128), (320, 128), (448, 64)]
    a1, a2, a3, a_total, a_finish = heads(
        a_product, a_chunks, 0, (a_acc_o, a_acc_s, a_ps_o, a_ps_s, a_pr_o, a_pr_s, a_xs, a_xr, a_ys, a_yr)
    )
    q1, q2, q3, q_total, q_finish = heads(
        q_product, q_chunks, 1, (q_acc_o, q_acc_s, q_ps_o, q_ps_s, q_pr_o, q_pr_s, q_xs, q_xr, q_ys, q_yr)
    )

    def kvl_copy(ch):
        s0, n = q_chunks[ch][0] // T, q_chunks[ch][1] // T
        return rcopy(
            kvl_part.at[pl.ds(s0, n), 1 - k], kvl_pair.at[pl.ds(s0, n)], kp_s.at[ch], kp_r.at[ch], mate
        )

    def kvl1(ch):
        s0, n = q_chunks[ch][0] // T, q_chunks[ch][1] // T
        rows = pl.ds(*q_chunks[ch])
        kvl_part[pl.ds(s0, n), :, :, pl.ds(0, 256)] = dot(nb[rows], wkv[...], 1, 0).reshape(n, 2, R, 256)
        kvl_part[pl.ds(s0, n), :, :, pl.ds(256, 256)] = dot(nb[rows], dwt[...], 1, 1).reshape(n, 2, R, 256)
        kvl_copy(ch).start()

    def to_chip(send, recv, s, n):
        @pl.when(s != c)
        def _():
            rcopy(send.at[s], recv.at[c], grp_s.at[n], grp_r.at[n], (d, 2 * s + k, t)).start()

    def kvl2(ch):
        s0, n = q_chunks[ch][0] // T, q_chunks[ch][1] // T
        kvl_copy(ch).wait_recv()
        for s in range(s0, s0 + n):
            kvl_send[s] = kvl_part[s, k] + kvl_pair[s]
            to_chip(kvl_send, kvl_recv, s, 5)

    def chip_total(own, recv):
        def add(i, total):
            return total + recv[lax.rem(c + i, NC)].astype(F32)

        return lax.fori_loop(1, NC, add, own)

    def gather_chips(buf, z, n):
        ref = buf.at[z, k]

        @pl.loop(1, NC)
        def _(i):
            rcopy(ref, ref, grp_s.at[n], grp_r.at[n], (d, 2 * lax.rem(c + i, NC) + k, t)).start()

    def gather_mate(buf, n):
        return rcopy(buf.at[:, k], buf.at[:, k], grp_s.at[n], grp_r.at[n], mate)

    def seven(buf):
        return buf.at[pl.ds(0, NC - 1), 0]

    def total_f(own, recv):
        def add(i, total):
            return total + recv[i].astype(F32)

        return lax.fori_loop(0, NF - 1, add, own.astype(F32))

    g_start(1)
    x_start(1)

    @pl.loop(1, NF)
    def _(i):
        rcopy(ss_own, ss_recv.at[i - 1], grp_s.at[0], grp_r.at[0], fdev(i)).start()

    copies[3].wait()
    a1(0, 0)
    a1(0, 1)
    a2(0)
    wait_bytes(ss_recv, grp_r.at[0])
    squares = total_f(ss_own[...], ss_recv)
    r_all[t] = lax.rsqrt(squares / (W * NF) + eps)

    @pl.loop(1, NT)
    def _(i):
        rcopy(r_all.at[t], r_all.at[t], grp_s.at[1], grp_r.at[1], zdev(i)).start()

    g_arrive(1)
    g_start(2)
    a1(1, 0)
    for i in (2, 4, 6, 7, 8, 9):
        copies[i].wait()
    x_arrive(1)
    x_start(2)
    a1(1, 1)
    wait_bytes(r_all.at[pl.ds(0, NT - 1)], grp_r.at[1])
    for slot in range(3):
        normalise(slot)
    kvl1(0)
    q1(0, 0)
    g_arrive(2)
    g_start(3)
    a2(1)
    a3(0)
    q1(0, 1)
    kvl2(0)
    a1(2, 0)
    x_arrive(2)
    x_start(3)
    a1(2, 1)
    q2(0)
    normalise(3)
    normalise(4)
    kvl1(1)
    q1(1, 0)
    g_arrive(3)
    g_start(4)
    q1(1, 1)
    a3(1)
    kvl2(1)
    a2(2)
    a1(3, 0)
    x_arrive(3)
    x_start(4)
    a1(3, 1)
    q2(1)
    q3(0)
    normalise(5)
    normalise(6)
    kvl1(2)
    q1(2, 0)
    g_arrive(4)
    kvl2(2)
    bo_part[...] = dot(gb[...], gup[...], 1, 1).astype(BF16)

    @pl.loop(1, NF)
    def _(i):
        fi = lax.rem(f + i, NF)
        rcopy(
            bo_part.at[pl.ds(pl.multiple_of(fi * R, R), R)], bo_recv.at[i - 1], grp_s.at[2], grp_r.at[2], (d, fi, t)
        ).start()

    a2(3)
    x_arrive(4)
    normalise(7)
    kvl1(3)
    q1(2, 1)
    kvl2(3)
    q1(3, 0)
    q2(2)
    q1(3, 1)
    a1(4, 0)
    q2(3)
    a1(4, 1)
    a3(2)
    q3(1)
    a2(4)
    a3(3)
    z_own = block(c)
    own_slots = pl.ds(pl.multiple_of(f * R, R), R)
    own_rows = pl.ds(pl.multiple_of(z_own * T + k * R, R), R)
    for i in range(11, 15):
        copies[i].wait()
    wait_bytes(kvl_recv.at[pl.ds(0, NC - 1)], grp_r.at[5])
    total = chip_total(kvl_send[c], kvl_recv)
    low = total[:, 256:].astype(BF16)
    keys = total[:, :H] + adapter_scale * dot(low, upk[...], 1, 0)
    values = total[:, H:256] + adapter_scale * dot(low, upv[...], 1, 0)
    keys = rotate(keys, cosb[own_rows], sinb[own_rows])
    kvl_all[z_own, k, :, pl.ds(0, H)] = keys.astype(BF16)
    kvl_all[z_own, k, :, pl.ds(H, H)] = values.astype(BF16)
    kvl_all[z_own, k, :, pl.ds(256, 256)] = low
    gather_chips(kvl_all, z_own, 6)
    wait_bytes(bo_recv, grp_r.at[2])
    bo_all[own_rows] = total_f(bo_part[own_slots], bo_recv).astype(BF16)
    bo_ref = bo_all.at[own_rows]

    @pl.loop(1, NF)
    def _(i):
        rcopy(bo_ref, bo_ref, grp_s.at[3], grp_r.at[3], fdev(i)).start()

    q3(2)
    q3(3)
    a3(4)
    wait_bytes(seven(kvl_all), grp_r.at[6])
    gather_mate(kvl_all, 7).start()

    def a_store(ch):
        value = a_total(ch)
        r0, size = a_chunks[ch]
        for s in range(r0 // T, (r0 + size) // T):
            part = value[s * T - r0 : (s + 1) * T - r0]
            rows = block_rows(s)
            dat[rows] = (part + adapter_scale * dot(bo_all[rows], odt[...], 1, 0)).astype(BF16)

    wait_bytes(bo_all.at[pl.ds(0, (NF - 1) * R)], grp_r.at[3])
    for ch in range(4):
        a_store(ch)
    gather_mate(kvl_all, 7).wait_recv()
    for ch, (r0, size) in enumerate(q_chunks):
        value = q_total(ch)
        for s in range(r0 // T, (r0 + size) // T):
            part = value[s * T - r0 : (s + 1) * T - r0]
            rows = block_rows(s)
            low = kvl_all[block(s), :, :, pl.ds(256, 256)].reshape(T, 256)
            query = part + adapter_scale * dot(low, upq[...], 1, 0)
            qrot[rows] = rotate(query, cosb[rows], sinb[rows]).astype(BF16)
    a_store(4)

    scale = 1.0 / math.sqrt(H)
    for i in range(4):
        rows = pl.ds(i * 128, 128)
        n = (i + 1) * 128
        seen = pl.ds(0, n)
        krot = kvl_all[pl.ds(0, n // T), :, :, pl.ds(0, H)].reshape(n, H)
        vals = kvl_all[pl.ds(0, n // T), :, :, pl.ds(H, H)].reshape(n, H)
        qi = qrot[rows]
        da = dat[rows]
        scores = dot(qi, krot, 1, 1) * scale
        causal = lax.broadcasted_iota(jnp.int32, (128, n), 0) + i * 128 >= lax.broadcasted_iota(
            jnp.int32, (128, n), 1
        )
        scores = jnp.where(causal, scores, -1e30)
        e = jnp.exp(scores - jnp.max(scores, axis=1, keepdims=True))
        probs = e / jnp.sum(e, axis=1, keepdims=True)
        probs_b = probs.astype(BF16)
        attn[rows] = dot(probs_b, vals, 1, 0).astype(BF16)
        dprobs = dot(da, vals, 1, 1)
        delta = jnp.sum(probs * dprobs, axis=1, keepdims=True)
        dscore = (probs * (dprobs - delta) * scale).astype(BF16)
        dquery = dot(dscore, krot, 1, 0)
        dq_own[rows] = rotate_back(dquery, cosb[rows], sinb[rows]).astype(BF16)
        dkacc[seen, pl.ds(0, H)] += dot(dscore, qi, 0, 0)
        dkacc[seen, pl.ds(H, H)] += dot(probs_b, da, 0, 0)

    z_chunks = [(448, 64), (320, 128), (192, 128), (0, 192)]

    def dqy_copy(ch, j):
        ref = dq_all.at[xl, y, k, pl.ds(*z_chunks[ch])]
        return rcopy(
            ref, ref, dqy_s.at[ch, j - 1], dqy_r.at[ch, j - 1], (d, 2 * (4 * xl + lax.rem(y + j, 4)) + k, t)
        )

    def dqx_copy(ch):
        ref = dq_all.at[xl, :, k, pl.ds(*z_chunks[ch])]
        return rcopy(ref, ref, dqx_s.at[ch], dqx_r.at[ch], xmate)

    def dqc_copy(ch, g):
        ref = dq_all.at[xl if g == 0 else 1 - xl, :, k, pl.ds(*z_chunks[ch])]
        return rcopy(ref, ref, dqc_s.at[ch, g], dqc_r.at[ch, g], mate)

    def dq_send(ch):
        r0, size = z_chunks[ch]
        for s in range(r0 // T, (r0 + size) // T):
            dq_all[xl, y, k, slot_rows(s)] = dq_own[block_rows(s)]
        for j in range(1, 4):
            dqy_copy(ch, j).start()

    def dq_forward_x(ch):
        for j in range(1, 4):
            dqy_copy(ch, j).wait_recv()
        dqx_copy(ch).start()
        dqc_copy(ch, 0).start()

    def dq_forward_core(ch):
        dqx_copy(ch).wait_recv()
        dqc_copy(ch, 1).start()

    dq_send(0)
    p1_part[:, :, :, pl.ds(0, 256)] = dkacc[...].reshape(NC, 2, R, 256)
    p1_part[:, :, :, pl.ds(256, H)] = (
        dot(dq_own[...], upq[pl.ds(0, H)], 1, 1) + dot(attn[...], odb[...], 1, 1)
    ).reshape(NC, 2, R, H)
    p1_copy = rcopy(p1_part.at[:, 1 - k], p1_pair, grp_s.at[8], grp_r.at[8], mate)
    p1_copy.start()
    sm_own[pl.ds(192, 64)] = dot(bo_all[...], attn[...], 0, 0)[:64]
    all_low = kvl_all[:, :, :, pl.ds(256, 256)].reshape(L, 256)
    sm_own[pl.ds(0, 64)] = dot(all_low, dq_own[...], 0, 0)[:64]
    p1_copy.wait_recv()
    for s in range(NC):
        p1_send[s] = (p1_part[s, k] + p1_pair[s]).astype(BF16)
        to_chip(p1_send, p1_recv, s, 9)
    dq_send(1)
    dq_forward_x(0)
    wait_bytes(p1_recv.at[pl.ds(0, NC - 1)], grp_r.at[9])
    total = chip_total(p1_part[c, k] + p1_pair[c], p1_recv)
    piece = pl.ds(pl.multiple_of(f * R, R), R)
    dkey = rotate_back(total[:, :H], cosb[piece], sinb[piece]).astype(BF16)
    dval = total[:, H:256].astype(BF16)
    dkv_all[c, k, :, pl.ds(0, H)] = dkey
    dkv_all[c, k, :, pl.ds(H, H)] = dval
    gather_chips(dkv_all, c, 10)
    p2_all[t, :, pl.ds(0, H)] = total[:, 256:].astype(BF16)
    p2_all[t, :, pl.ds(H, H)] = (
        dot(dkey, upk[pl.ds(H, H)], 1, 1) + dot(dval, upv[pl.ds(H, H)], 1, 1)
    ).astype(BF16)

    @pl.loop(1, NT)
    def _(i):
        rcopy(p2_all.at[t], p2_all.at[t], grp_s.at[12], grp_r.at[12], zdev(i)).start()

    dq_send(2)
    dq_send(3)
    dq_forward_x(1)
    wait_bytes(seven(dkv_all), grp_r.at[10])
    gather_mate(dkv_all, 11).start()
    dq_forward_core(0)
    wait_bytes(p2_all.at[pl.ds(0, NT - 1)], grp_r.at[12])
    total = p2_all[0].astype(F32)
    for i in range(1, NT):
        total = total + p2_all[i].astype(F32)
    back_all[c, k] = total.astype(BF16)
    gather_chips(back_all, c, 13)
    dq_forward_x(2)
    dq_forward_core(1)
    gather_mate(dkv_all, 11).wait_recv()
    for s in range(NT):
        dkv_slot[slot_rows(s)] = dkv_all[block(s)].reshape(T, 256)

    def slots_of(j, way):
        far = ([7, 5, 3, 1], [7, 6, 4, 2])[way]
        return far if j % 2 == way else far[1:]

    def rs_copy(j, way, s):
        send, recv = ((rs_sendr, rs_recvr), (rs_sendl, rs_recvl))[way]
        return rcopy(
            send.at[j, s], recv.at[j, s], rs_s.at[way, j, s], rs_r.at[way, j, s], zdev(1 - 2 * way)
        )

    def rs_step(j, way, s):
        value = zpart[j, slot_rows(slots_of(j, way)[s])]
        send, recv = ((rs_sendr, rs_recvr), (rs_sendl, rs_recvl))[way]
        if s > 0:
            rs_copy(j, way, s - 1).wait_recv()
            value = value + recv[j, s - 1].astype(F32)
        send[j, s] = value.astype(BF16)
        rs_copy(j, way, s).start()

    def z_products(ch):
        rows = pl.ds(*z_chunks[ch])
        dqc_copy(ch, 0).wait_recv()
        dqc_copy(ch, 1).wait_recv()
        dq = jnp.concatenate([dq_all[i // 8, i // 2 % 4, i % 2, rows] for i in range(NF)], axis=1)
        for j in range(4):
            wide = pl.ds(j * 256, 256)
            zpart[j, rows] = dot(dq, wq[wide, :], 1, 1) + dot(dkv_slot[rows], wkv[wide, :], 1, 1)
            for way in range(2):
                s = ch if j % 2 == way else ch - 1
                if s >= 0:
                    rs_step(j, way, s)

    z_products(0)
    dq_forward_x(3)
    wait_bytes(seven(back_all), grp_r.at[13])
    gather_mate(back_all, 14).start()
    z_products(1)
    gather_mate(back_all, 14).wait_recv()
    for s in range(NT):
        back_slot[slot_rows(s)] = back_all[block(s)].reshape(T, 256)
    halves = []
    for i in range(2):
        rows = pl.ds(i * 128, 128)
        ex_own[rows] = dot(back_slot[:, rows], nb[...], 0, 0).astype(BF16)
        if i == 0:
            ex_own[pl.ds(64, 64)] = dot(back_slot[:, rows], gb[...], 0, 0)[64:].astype(BF16)
        halves.append(rcopy(ex_own.at[rows], ex_recv.at[rows], dp_s.at[1 + i], dp_r.at[1 + i], other))
        halves[i].start()
    dq_forward_core(2)
    z_products(2)
    dq_forward_core(3)
    kv_up = dot(all_low, dkv_all[...].reshape(L, 256), 0, 0)
    sm_own[pl.ds(64, 64)] = kv_up[128:192, :H]
    sm_own[pl.ds(128, 64)] = kv_up[192:, H:]
    small = rcopy(sm_own, sm_recv, dp_s.at[0], dp_r.at[0], other)
    small.start()
    z_products(3)

    inverse = column(r_all[t])
    xhat = x_own * inverse
    dhat = []
    for j in range(4):
        wide = pl.ds(j * 256, 256)
        value = zpart[j, slot_rows(0)] + adapter_scale * dot(back_slot[slot_rows(0)], dwt[:, wide], 1, 0)
        for way, recv in enumerate((rs_recvr, rs_recvl)):
            last = len(slots_of(j, way)) - 1
            rs_copy(j, way, last).wait_recv()
            value = value + recv[j, last].astype(F32)
        dhat.append(value)
    dhat = jnp.concatenate(dhat, axis=1) * gain_row()
    inner = dot(ones, dhat * xhat, 1, 1, precision=lax.Precision.HIGHEST)
    ip_own[...] = jnp.concatenate([inner, inner], axis=1)

    @pl.loop(1, NF)
    def _(i):
        rcopy(ip_own, ip_recv.at[i - 1], grp_s.at[15], grp_r.at[15], fdev(i)).start()

    small.wait_recv()
    both = adapter_scale * (sm_own[...] + sm_recv[...])
    sm_o[pl.ds(0, 64)] = both[:64]
    sm_o[pl.ds(64, 64, stride=2)] = both[64:128]
    sm_o[pl.ds(65, 64, stride=2)] = both[128:192]
    sm_o[pl.ds(192, 64)] = both[192:]
    wait_bytes(ip_recv, grp_r.at[15])
    inner = total_f(ip_own[...], ip_recv) / (W * NF)
    hid_o[...] = gb[slot_rows(0)].astype(F32) + inverse * (dhat - xhat * column(inner))
    halves[0].wait_recv()

    def added(i, n):
        return adapter_scale * (ex_own[pl.ds(i, n)].astype(F32) + ex_recv[pl.ds(i, n)].astype(F32))

    pd_o[pl.ds(0, 64)] = added(0, 64)
    ou_o[...] = added(64, 64)
    halves[1].wait_recv()
    pd_o[pl.ds(64, 128)] = added(128, 128)

    g_finish()
    x_finish()
    a_finish()
    q_finish()
    for ch in range(4):
        kvl_copy(ch).wait_send()
        dqx_copy(ch).wait_send()
        dqc_copy(ch, 0).wait_send()
        dqc_copy(ch, 1).wait_send()
        for j in range(1, 4):
            dqy_copy(ch, j).wait_send()
    for j in range(4):
        for way in range(2):
            for s in range(len(slots_of(j, way))):
                rs_copy(j, way, s).wait_send()
    p1_copy.wait_send()
    small.wait_send()
    for half in halves:
        half.wait_send()
    gather_mate(kvl_all, 7).wait_send()
    gather_mate(dkv_all, 11).wait_send()
    gather_mate(back_all, 14).wait_send()
    sent = {
        0: ss_recv, 1: r_all.at[pl.ds(0, NT - 1)], 2: bo_recv, 3: bo_all.at[pl.ds(0, (NF - 1) * R)],
        5: kvl_recv.at[pl.ds(0, NC - 1)], 6: seven(kvl_all), 9: p1_recv.at[pl.ds(0, NC - 1)], 10: seven(dkv_all),
        12: p2_all.at[pl.ds(0, NT - 1)], 13: seven(back_all), 15: ip_recv,
    }
    for n, ref in sent.items():
        wait_bytes(ref, grp_s.at[n])


def hand_over(hid, pd, ou, sm, hid_o, pd_o, ou_o, qu_o, ku_o, od_o):
    hid_o[...] = hid[...]
    pd_o[...] = pd[...]
    ou_o[...] = ou[...]
    qu_o[...] = sm[pl.ds(0, 64)]
    ku_o[...] = sm[pl.ds(64, 128)]
    od_o[...] = sm[pl.ds(192, 64)]


def local(
    residual_input,
    block_output_gradient,
    norm_gain_vector,
    query_matrix,
    keyvalue_matrix,
    output_matrix,
    adapter_projection_down,
    adapter_query_up,
    adapter_keyvalue_up,
    adapter_output_down,
    adapter_output_up,
):
    cosine, sine = rope_tables()
    vm = pltpu.VMEM
    dma = pltpu.SemaphoreType.DMA
    quarter = [vm((4, L, H), BF16)] * 7 + [vm((3, L, H), BF16)]
    heads = [vm((4, L, H), F32)] * 2 + quarter
    scratch = [
        vm((L, W), BF16), vm((L, W), BF16), vm((L, W), BF16),
        vm((W, 2048), BF16), vm((2048, W), BF16), vm((W, 256), BF16), vm((256, W), BF16), vm((128, W), BF16),
        vm((256, H), BF16), vm((256, H), BF16), vm((256, H), BF16), vm((128, H), BF16), vm((128, H), BF16),
        vm((8, H), F32), vm((L, H), F32), vm((L, H), F32),
        vm((2 * W, H), BF16), vm((2 * W, H), F32), vm((128, H), BF16), vm((128, H), F32),
        vm((8, H), F32), vm((NF - 1, 8, H), F32), vm((NT, 8, H), F32), vm((8, H), F32), vm((NF - 1, 8, H), F32),
        vm((L, H), BF16), vm((NF - 1, R, H), BF16), vm((L, H), BF16),
        vm((NC, 2, R, 512), F32), vm((NC, R, 512), F32), vm((NC, R, 512), F32), vm((NC, R, 512), F32),
        vm((NC, 2, R, 512), BF16),
        *heads, *heads,
        vm((L, H), BF16), vm((L, H), BF16), vm((L, H), BF16), vm((L, H), BF16), vm((2, 4, 2, L, H), BF16),
        vm((L, 256), F32),
        vm((NC, 2, R, 384), F32), vm((NC, R, 384), F32), vm((NC, R, 384), BF16), vm((NC, R, 384), BF16),
        vm((NC, 2, R, 256), BF16), vm((L, 256), BF16), vm((NT, R, 256), BF16),
        vm((NC, 2, R, 256), BF16), vm((L, 256), BF16),
        vm((4, L, 256), F32),
        vm((4, 4, T, 256), BF16), vm((4, 4, T, 256), BF16), vm((4, 4, T, 256), BF16), vm((4, 4, T, 256), BF16),
        vm((256, H), F32), vm((256, H), F32), vm((256, W), BF16), vm((256, W), BF16),
        dma((16,)), dma((16,)), dma((16,)), dma((2, 2, 4)), dma((2, 2, 4)), dma((4,)), dma((4,)),
        dma((2, 5, 2)), dma((2, 5, 2)), dma((2, 5)), dma((2, 5)), dma((2, 5, 3)), dma((2, 5, 3)),
        dma((4, 3)), dma((4, 3)), dma((4,)), dma((4,)), dma((4, 2)), dma((4, 2)),
        dma((2, 4, 4)), dma((2, 4, 4)), dma((3,)), dma((3,)),
    ]
    hidden, down, up, small = pl.pallas_call(
        kernel,
        out_shape=(
            jax.ShapeDtypeStruct((T, W), F32),
            jax.ShapeDtypeStruct((192, W), F32),
            jax.ShapeDtypeStruct((64, W), F32),
            jax.ShapeDtypeStruct((256, H), F32),
        ),
        in_specs=[pl.BlockSpec(memory_space=pl.ANY)] * 13,
        out_specs=(pl.BlockSpec(memory_space=pltpu.VMEM),) * 4,
        scratch_shapes=scratch,
        compiler_params=pltpu.CompilerParams(
            collective_id=0, has_side_effects=True, vmem_limit_bytes=60 * 2**20
        ),
        name="adapter_backward",
    )(
        residual_input[0],
        block_output_gradient[0],
        norm_gain_vector.reshape(8, H),
        query_matrix[:, 0, :],
        output_matrix[0],
        keyvalue_matrix.reshape(2 * W, H),
        adapter_projection_down.T,
        adapter_output_up,
        adapter_query_up[:, 0, :],
        adapter_keyvalue_up.reshape(128, H),
        adapter_output_down[0].T,
        jnp.asarray(cosine),
        jnp.asarray(sine),
    )
    hidden, down, up, query_up, keyvalue_up, output_down = pl.pallas_call(
        hand_over,
        out_shape=(
            jax.ShapeDtypeStruct((T, W), F32),
            jax.ShapeDtypeStruct((192, W), F32),
            jax.ShapeDtypeStruct((64, W), F32),
            jax.ShapeDtypeStruct((64, H), F32),
            jax.ShapeDtypeStruct((128, H), F32),
            jax.ShapeDtypeStruct((64, H), F32),
        ),
        in_specs=[pl.BlockSpec(memory_space=pltpu.VMEM)] * 4,
        out_specs=(pl.BlockSpec(memory_space=pltpu.VMEM),) * 6,
        name="hand_over",
    )(hidden, down, up, small)
    return (
        hidden[None],
        down.T,
        query_up[:, None, :],
        keyvalue_up.reshape(64, 2, H),
        output_down.T[None],
        up,
    )


def solution(mesh):
    in_specs = (
        P("dp", "tensor", "fsdp"),
        P("dp", "tensor", "fsdp"),
        P("fsdp"),
        P("fsdp", "tensor", None),
        P("fsdp", None, "tensor"),
        P("tensor", None, "fsdp"),
        P("fsdp", None),
        P(None, "tensor", "fsdp"),
        P(None, None, "tensor"),
        P("tensor", "fsdp", None),
        P(None, "fsdp"),
    )
    out_specs = (
        P("dp", "tensor", "fsdp"),
        P("fsdp", None),
        P(None, "tensor", "fsdp"),
        P(None, None, "tensor"),
        P("tensor", "fsdp", None),
        P(None, "fsdp"),
    )
    return jax.shard_map(local, mesh=mesh, in_specs=in_specs, out_specs=out_specs, check_vma=False)
```

```python
import math

import jax
import jax.numpy as jnp
import numpy as np
from jax import lax
from jax.experimental import pallas as pl
from jax.experimental.pallas import tpu as pltpu
from jax.sharding import PartitionSpec as P

eps = 1e-05
adapter_scale = 2.0
theta = 500000.0
MESH = pl.DeviceIdType.MESH
F32 = jnp.float32
BF16 = jnp.bfloat16

NF = 16
NC = 8
NT = 8
L = 512
T = 64
W = 1024
H = 128
R = 32


def rope_tables():
    half = H // 2
    freq = np.float32(theta) ** (-(np.arange(half, dtype=np.float32) * np.float32(2.0)) / np.float32(H))
    angles = np.arange(L, dtype=np.float32)[:, None] * freq[None, :].astype(np.float32)
    angles = angles.astype(np.float64)
    cosine, sine = np.cos(angles), np.sin(angles)
    return (
        np.concatenate([cosine, cosine], axis=1).astype(np.float32),
        np.concatenate([-sine, sine], axis=1).astype(np.float32),
    )


def dot(a, b, ca, cb, **kw):
    return lax.dot_general(a, b, (((ca,), (cb,)), ((), ())), preferred_element_type=F32, **kw)


def rotate(v, c, s):
    return v * c + pltpu.roll(v, H // 2, axis=1) * s


def rotate_back(v, c, s):
    return v * c - pltpu.roll(v, H // 2, axis=1) * s


def kernel(
    x_h, g_h, gain_h, wq_h, wo_h, wkv_h, dwt_h, gup_h, upq_h, upkv_h, odt_h, cos_h, sin_h,
    hid_o, pd_o, ou_o, sm_o,
    xb, gb, nb, wq, wo, wkv, dwt, gup, upq, upk, upv, odt, odb, gain, cosb, sinb, wkv_in, wkv_f, upkv_in, upkv_f,
    ss_own, ss_recv, r_all, ip_own, ip_recv, bo_part, bo_recv, bo_all,
    kvl_part, kvl_pair, kvl_send, kvl_recv, kvl_all,
    a_acc_o, a_acc_s, a_ps_o, a_ps_s, a_pr_o, a_pr_s, a_xs, a_xr, a_ys, a_yr,
    q_acc_o, q_acc_s, q_ps_o, q_ps_s, q_pr_o, q_pr_s, q_xs, q_xr, q_ys, q_yr,
    qrot, dat, attn, dq_own, dq_all, dkacc,
    p1_part, p1_pair, p1_send, p1_recv, dkv_all, dkv_slot, p2_all, back_all, back_slot,
    zpart, rs_sendr, rs_recvr, rs_sendl, rs_recvl, sm_own, sm_recv, ex_own, ex_recv,
    ld, grp_s, grp_r, ring_s, ring_r, kp_s, kp_r, pair_s, pair_r, xm_s, xm_r, yy_s, yy_r,
    dqy_s, dqy_r, dqx_s, dqx_r, dqc_s, dqc_r, rs_s, rs_r, dp_s, dp_r,
):
    d = lax.axis_index("dp")
    f = lax.axis_index("fsdp")
    t = lax.axis_index("tensor")
    c = f // 2
    k = f % 2
    xl = c // 4
    y = c % 4

    def rcopy(src, dst, ss, rs, dev):
        return pltpu.make_async_remote_copy(
            src_ref=src, dst_ref=dst, send_sem=ss, recv_sem=rs, device_id=dev, device_id_type=MESH
        )

    def wait_bytes(ref, sem):
        pltpu.make_async_copy(ref, ref, sem).wait()

    def fdev(i):
        return (d, lax.rem(f + i, NF), t)

    def zdev(i):
        return (d, f, lax.rem(t + i + NT, NT))

    mate = (d, 2 * c + 1 - k, t)
    xmate = (d, 2 * (4 * (1 - xl) + y) + k, t)
    other = (1 - d, f, t)

    def block(slot):
        rel = jnp.where(slot % 2 == 1, (slot + 1) // 2, NT - slot // 2) if not isinstance(slot, int) else (
            (slot + 1) // 2 if slot % 2 == 1 else NT - slot // 2
        )
        return lax.rem(t + rel, NT)

    def block_rows(slot):
        return pl.ds(pl.multiple_of(block(slot) * T, T), T)

    def slot_rows(slot):
        return pl.ds(slot * T, T)

    loads = [
        (g_h, gb.at[slot_rows(0)]),
        (x_h, xb.at[slot_rows(0)]),
        (gain_h, gain),
        (wo_h, wo),
        (wq_h, wq),
        (wkv_h, wkv_in),
        (dwt_h.at[pl.ds(0, 64)], dwt.at[pl.ds(0, 64)]),
        (dwt_h.at[pl.ds(64, 128)], dwt.at[pl.ds(128, 128)]),
        (gup_h, gup.at[pl.ds(0, 64)]),
        (upq_h, upq.at[pl.ds(0, 64)]),
        (upkv_h, upkv_in),
        (odt_h, odt.at[pl.ds(0, 64)]),
        (odt_h, odb.at[pl.ds(64, 64)]),
        (cos_h, cosb),
        (sin_h, sinb),
    ]
    copies = [pltpu.make_async_copy(s, o, ld.at[i]) for i, (s, o) in enumerate(loads)]
    for copy in copies:
        copy.start()

    barrier = pltpu.get_barrier_semaphore()

    @pl.loop(1, NF)
    def _(i):
        pl.semaphore_signal(barrier, inc=1, device_id=fdev(i), device_id_type=MESH)

    @pl.loop(1, NT)
    def _(i):
        pl.semaphore_signal(barrier, inc=1, device_id=zdev(i), device_id_type=MESH)

    pl.semaphore_signal(barrier, inc=1, device_id=other, device_id_type=MESH)

    dwt[pl.ds(64, 64)] = jnp.zeros((64, W), BF16)
    gup[pl.ds(64, 64)] = jnp.zeros((64, W), BF16)
    upq[pl.ds(64, 192)] = jnp.zeros((192, H), BF16)
    upk[pl.ds(0, 128)] = jnp.zeros((128, H), BF16)
    upk[pl.ds(192, 64)] = jnp.zeros((64, H), BF16)
    upv[pl.ds(0, 192)] = jnp.zeros((192, H), BF16)
    odt[pl.ds(64, 64)] = jnp.zeros((64, H), BF16)
    odb[pl.ds(0, 64)] = jnp.zeros((64, H), BF16)
    dkacc[...] = jnp.zeros_like(dkacc)
    copies[0].wait()
    copies[1].wait()
    x_own = xb[slot_rows(0)].astype(F32)
    ones = jnp.ones((8, W), F32)
    squares = dot(ones, x_own * x_own, 1, 1, precision=lax.Precision.HIGHEST)
    ss_own[...] = jnp.concatenate([squares, squares], axis=1)

    copies[5].wait()
    copies[10].wait()
    wkv_f[...] = wkv_in[...].astype(F32)
    wkv[:, pl.ds(0, H)] = wkv_f[pl.ds(0, W, stride=2)].astype(BF16)
    wkv[:, pl.ds(H, H)] = wkv_f[pl.ds(1, W, stride=2)].astype(BF16)
    upkv_f[...] = upkv_in[...].astype(F32)
    upk[pl.ds(128, 64)] = upkv_f[pl.ds(0, 64, stride=2)].astype(BF16)
    upv[pl.ds(192, 64)] = upkv_f[pl.ds(1, 64, stride=2)].astype(BF16)
    pl.semaphore_wait(barrier, NF - 1 + NT - 1 + 1)

    def ring(buf, n):
        def right(s):
            src, dst = (0, 2, 4, 6)[s - 1], (2, 4, 6, 7)[s - 1]
            size = T if s < 4 else T // 2
            return rcopy(
                buf.at[pl.ds(src * T, size)], buf.at[pl.ds(dst * T, size)],
                ring_s.at[n, 0, s - 1], ring_r.at[n, 0, s - 1], zdev(1),
            )

        def left(s):
            src, dst = (0, 1, 3, 5)[s - 1], (1, 3, 5, 7)[s - 1]
            size, off = (T, 0) if s < 4 else (T // 2, T // 2)
            return rcopy(
                buf.at[pl.ds(src * T + off, size)], buf.at[pl.ds(dst * T + off, size)],
                ring_s.at[n, 1, s - 1], ring_r.at[n, 1, s - 1], zdev(-1),
            )

        def start(s):
            right(s).start()
            left(s).start()

        def arrive(s):
            right(s).wait_recv()
            left(s).wait_recv()

        def finish(last=4):
            for s in range(1, last + 1):
                right(s).wait_send()
                left(s).wait_send()

        return start, arrive, finish

    g_start, g_arrive, g_finish = ring(gb, 0)
    x_start, x_arrive, x_finish = ring(xb, 1)

    def column(rows8):
        return rows8.T[:T, 0:1]

    def gain_row():
        return jnp.concatenate([gain[pl.ds(i, 1)] for i in range(8)], axis=1)

    def normalise(slot):
        rows = slot_rows(slot)
        nb[rows] = (xb[rows].astype(F32) * column(r_all[block(slot)]) * gain_row()).astype(BF16)

    def heads(product, chunks, n, bufs):
        acc_o, acc_s, ps_o, ps_s, pr_o, pr_s, xs, xr, ys, yr = bufs

        def rows_of(ch):
            return pl.ds(*chunks[ch])

        def pair_copy(ch, g):
            src, dst = ((ps_o, pr_o), (ps_s, pr_s))[g]
            return rcopy(src.at[:, rows_of(ch)], dst.at[:, rows_of(ch)], pair_s.at[n, ch, g], pair_r.at[n, ch, g], mate)

        def x_copy(ch):
            return rcopy(xs.at[:, rows_of(ch)], xr.at[:, rows_of(ch)], xm_s.at[n, ch], xm_r.at[n, ch], xmate)

        def y_copy(ch, j):
            yj = lax.rem(y + j, 4)
            return rcopy(
                ys.at[yj, rows_of(ch)], yr.at[j - 1, rows_of(ch)], yy_s.at[n, ch, j - 1], yy_r.at[n, ch, j - 1],
                (d, 2 * (4 * xl + yj) + k, t),
            )

        def first(ch, g):
            rows = rows_of(ch)
            acc, ps = ((acc_o, ps_o), (acc_s, ps_s))[g]
            base = 4 * (1 - xl) if g == 0 else 4 * xl

            @pl.loop(0, 4)
            def _(i):
                both = product(rows, base + i)
                acc[i, rows] = jnp.where(k == 0, both[:, :H], both[:, H:])
                ps[i, rows] = jnp.where(k == 0, both[:, H:], both[:, :H]).astype(BF16)

            pair_copy(ch, g).start()

        def second(ch):
            rows = rows_of(ch)
            pair_copy(ch, 0).wait_recv()

            @pl.loop(0, 4)
            def _(i):
                xs[i, rows] = (acc_o[i, rows] + pr_o[i, rows].astype(F32)).astype(BF16)

            x_copy(ch).start()

        def third(ch):
            rows = rows_of(ch)
            pair_copy(ch, 1).wait_recv()
            x_copy(ch).wait_recv()
            for j in range(1, 4):
                yj = lax.rem(y + j, 4)
                ys[yj, rows] = (acc_s[yj, rows] + pr_s[yj, rows].astype(F32) + xr[yj, rows].astype(F32)).astype(BF16)
                y_copy(ch, j).start()

        def total(ch):
            rows = rows_of(ch)
            value = acc_s[y, rows] + pr_s[y, rows].astype(F32) + xr[y, rows].astype(F32)
            for j in range(1, 4):
                y_copy(ch, j).wait_recv()
                value = value + yr[j - 1, rows].astype(F32)
            return value

        def finish():
            for ch in range(len(chunks)):
                pair_copy(ch, 0).wait_send()
                pair_copy(ch, 1).wait_send()
                x_copy(ch).wait_send()
                for j in range(1, 4):
                    y_copy(ch, j).wait_send()

        return first, second, third, total, finish

    def a_product(rows, ci):
        return dot(gb[rows], wo[pl.ds(pl.multiple_of(ci * 256, 256), 256), :], 1, 1)

    def q_product(rows, ci):
        return dot(nb[rows], wq[:, pl.ds(pl.multiple_of(ci * 256, 256), 256)], 1, 0)

    a_chunks = [(0, 64), (64, 128), (192, 128), (320, 128), (448, 64)]
    q_chunks = [(0, 192), (192, 128), (320, 128), (448, 64)]
    a1, a2, a3, a_total, a_finish = heads(
        a_product, a_chunks, 0, (a_acc_o, a_acc_s, a_ps_o, a_ps_s, a_pr_o, a_pr_s, a_xs, a_xr, a_ys, a_yr)
    )
    q1, q2, q3, q_total, q_finish = heads(
        q_product, q_chunks, 1, (q_acc_o, q_acc_s, q_ps_o, q_ps_s, q_pr_o, q_pr_s, q_xs, q_xr, q_ys, q_yr)
    )

    def kvl_copy(ch):
        s0, n = q_chunks[ch][0] // T, q_chunks[ch][1] // T
        return rcopy(
            kvl_part.at[pl.ds(s0, n), 1 - k], kvl_pair.at[pl.ds(s0, n)], kp_s.at[ch], kp_r.at[ch], mate
        )

    def kvl1(ch):
        s0, n = q_chunks[ch][0] // T, q_chunks[ch][1] // T
        rows = pl.ds(*q_chunks[ch])
        kvl_part[pl.ds(s0, n), :, :, pl.ds(0, 256)] = dot(nb[rows], wkv[...], 1, 0).reshape(n, 2, R, 256)
        kvl_part[pl.ds(s0, n), :, :, pl.ds(256, 256)] = dot(nb[rows], dwt[...], 1, 1).reshape(n, 2, R, 256)
        kvl_copy(ch).start()

    def to_chip(send, recv, s, n, chip):
        @pl.when(chip != c)
        def _():
            rcopy(send.at[s], recv.at[c], grp_s.at[n], grp_r.at[n], (d, 2 * chip + k, t)).start()

    def kvl2(ch):
        s0, n = q_chunks[ch][0] // T, q_chunks[ch][1] // T
        kvl_copy(ch).wait_recv()
        for s in range(s0, s0 + n):
            kvl_send[s] = kvl_part[s, k] + kvl_pair[s]
            to_chip(kvl_send, kvl_recv, s, 5, lax.rem(s + 4 * k, NC))

    def chip_total(own, recv):
        def add(i, total):
            return total + recv[lax.rem(c + i, NC)].astype(F32)

        return lax.fori_loop(1, NC, add, own)

    def gather_chips(buf, z, n):
        ref = buf.at[z, k]

        @pl.loop(1, NC)
        def _(i):
            rcopy(ref, ref, grp_s.at[n], grp_r.at[n], (d, 2 * lax.rem(c + i, NC) + k, t)).start()

    def gather_mate(buf, n):
        return rcopy(buf.at[:, k], buf.at[:, k], grp_s.at[n], grp_r.at[n], mate)

    def seven(buf):
        return buf.at[pl.ds(0, NC - 1), 0]

    def total_f(own, recv):
        def add(i, total):
            return total + recv[i].astype(F32)

        return lax.fori_loop(0, NF - 1, add, own.astype(F32))

    g_start(1)
    x_start(1)

    @pl.loop(1, NF)
    def _(i):
        rcopy(ss_own, ss_recv.at[i - 1], grp_s.at[0], grp_r.at[0], fdev(i)).start()

    copies[3].wait()
    a1(0, 0)
    a1(0, 1)
    a2(0)
    wait_bytes(ss_recv, grp_r.at[0])
    squares = total_f(ss_own[...], ss_recv)
    r_all[t] = lax.rsqrt(squares / (W * NF) + eps)

    @pl.loop(1, NT)
    def _(i):
        rcopy(r_all.at[t], r_all.at[t], grp_s.at[1], grp_r.at[1], zdev(i)).start()

    g_arrive(1)
    g_start(2)
    a1(1, 0)
    for i in (2, 4, 6, 7, 8, 9):
        copies[i].wait()
    x_arrive(1)
    x_start(2)
    a1(1, 1)
    wait_bytes(r_all.at[pl.ds(0, NT - 1)], grp_r.at[1])
    for slot in range(3):
        normalise(slot)
    kvl1(0)
    q1(0, 0)
    g_arrive(2)
    g_start(3)
    a2(1)
    a3(0)
    q1(0, 1)
    kvl2(0)
    a1(2, 0)
    x_arrive(2)
    x_start(3)
    a1(2, 1)
    q2(0)
    normalise(3)
    normalise(4)
    kvl1(1)
    q1(1, 0)
    g_arrive(3)
    g_start(4)
    q1(1, 1)
    a3(1)
    kvl2(1)
    a2(2)
    a1(3, 0)
    x_arrive(3)
    x_start(4)
    a1(3, 1)
    q2(1)
    q3(0)
    normalise(5)
    normalise(6)
    kvl1(2)
    q1(2, 0)
    g_arrive(4)
    kvl2(2)
    bo_part[...] = dot(gb[...], gup[...], 1, 1).astype(BF16)

    @pl.loop(1, NF)
    def _(i):
        fi = lax.rem(f + i, NF)
        rcopy(
            bo_part.at[pl.ds(pl.multiple_of(fi * R, R), R)], bo_recv.at[i - 1], grp_s.at[2], grp_r.at[2], (d, fi, t)
        ).start()

    a2(3)
    x_arrive(4)
    normalise(7)
    kvl1(3)
    q1(2, 1)
    kvl2(3)
    q1(3, 0)
    q2(2)
    q1(3, 1)
    a1(4, 0)
    q2(3)
    a1(4, 1)
    a3(2)
    q3(1)
    a2(4)
    a3(3)
    own_slots = pl.ds(pl.multiple_of(f * R, R), R)
    bo_rows = pl.ds(pl.multiple_of(block(c) * T + k * R, R), R)
    kv_slot = lax.rem(c + 4 * k, NC)
    z_own = block(kv_slot)
    own_rows = pl.ds(pl.multiple_of(z_own * T + k * R, R), R)
    for i in range(11, 15):
        copies[i].wait()
    wait_bytes(kvl_recv.at[pl.ds(0, NC - 1)], grp_r.at[5])
    total = chip_total(kvl_send[kv_slot], kvl_recv)
    low = total[:, 256:].astype(BF16)
    keys = total[:, :H] + adapter_scale * dot(low, upk[...], 1, 0)
    values = total[:, H:256] + adapter_scale * dot(low, upv[...], 1, 0)
    keys = rotate(keys, cosb[own_rows], sinb[own_rows])
    kvl_all[z_own, k, :, pl.ds(0, H)] = keys.astype(BF16)
    kvl_all[z_own, k, :, pl.ds(H, H)] = values.astype(BF16)
    kvl_all[z_own, k, :, pl.ds(256, 256)] = low
    gather_chips(kvl_all, z_own, 6)
    wait_bytes(bo_recv, grp_r.at[2])
    bo_all[bo_rows] = total_f(bo_part[own_slots], bo_recv).astype(BF16)
    bo_ref = bo_all.at[bo_rows]

    @pl.loop(1, NF)
    def _(i):
        rcopy(bo_ref, bo_ref, grp_s.at[3], grp_r.at[3], fdev(i)).start()

    q3(2)
    q3(3)
    a3(4)
    wait_bytes(seven(kvl_all), grp_r.at[6])
    gather_mate(kvl_all, 7).start()

    def a_store(ch):
        value = a_total(ch)
        r0, size = a_chunks[ch]
        for s in range(r0 // T, (r0 + size) // T):
            part = value[s * T - r0 : (s + 1) * T - r0]
            rows = block_rows(s)
            dat[rows] = (part + adapter_scale * dot(bo_all[rows], odt[...], 1, 0)).astype(BF16)

    wait_bytes(bo_all.at[pl.ds(0, (NF - 1) * R)], grp_r.at[3])
    for ch in range(4):
        a_store(ch)
    gather_mate(kvl_all, 7).wait_recv()
    for ch, (r0, size) in enumerate(q_chunks):
        value = q_total(ch)
        for s in range(r0 // T, (r0 + size) // T):
            part = value[s * T - r0 : (s + 1) * T - r0]
            rows = block_rows(s)
            low = kvl_all[block(s), :, :, pl.ds(256, 256)].reshape(T, 256)
            query = part + adapter_scale * dot(low, upq[...], 1, 0)
            qrot[rows] = rotate(query, cosb[rows], sinb[rows]).astype(BF16)
    a_store(4)

    scale = 1.0 / math.sqrt(H)
    for i in range(4):
        rows = pl.ds(i * 128, 128)
        n = (i + 1) * 128
        seen = pl.ds(0, n)
        krot = kvl_all[pl.ds(0, n // T), :, :, pl.ds(0, H)].reshape(n, H)
        vals = kvl_all[pl.ds(0, n // T), :, :, pl.ds(H, H)].reshape(n, H)
        qi = qrot[rows]
        da = dat[rows]
        scores = dot(qi, krot, 1, 1) * scale
        causal = lax.broadcasted_iota(jnp.int32, (128, n), 0) + i * 128 >= lax.broadcasted_iota(
            jnp.int32, (128, n), 1
        )
        scores = jnp.where(causal, scores, -1e30)
        e = jnp.exp(scores - jnp.max(scores, axis=1, keepdims=True))
        probs = e / jnp.sum(e, axis=1, keepdims=True)
        probs_b = probs.astype(BF16)
        attn[rows] = dot(probs_b, vals, 1, 0).astype(BF16)
        dprobs = dot(da, vals, 1, 1)
        delta = jnp.sum(probs * dprobs, axis=1, keepdims=True)
        dscore = (probs * (dprobs - delta) * scale).astype(BF16)
        dquery = dot(dscore, krot, 1, 0)
        dq_own[rows] = rotate_back(dquery, cosb[rows], sinb[rows]).astype(BF16)
        dkacc[seen, pl.ds(0, H)] += dot(dscore, qi, 0, 0)
        dkacc[seen, pl.ds(H, H)] += dot(probs_b, da, 0, 0)

    z_chunks = [(448, 64), (320, 128), (192, 128), (0, 192)]

    def dqy_copy(ch, j):
        ref = dq_all.at[xl, y, k, pl.ds(*z_chunks[ch])]
        return rcopy(
            ref, ref, dqy_s.at[ch, j - 1], dqy_r.at[ch, j - 1], (d, 2 * (4 * xl + lax.rem(y + j, 4)) + k, t)
        )

    def dqx_copy(ch):
        ref = dq_all.at[xl, :, k, pl.ds(*z_chunks[ch])]
        return rcopy(ref, ref, dqx_s.at[ch], dqx_r.at[ch], xmate)

    def dqc_copy(ch, g):
        ref = dq_all.at[xl if g == 0 else 1 - xl, :, k, pl.ds(*z_chunks[ch])]
        return rcopy(ref, ref, dqc_s.at[ch, g], dqc_r.at[ch, g], mate)

    def dq_send(ch):
        r0, size = z_chunks[ch]
        for s in range(r0 // T, (r0 + size) // T):
            dq_all[xl, y, k, slot_rows(s)] = dq_own[block_rows(s)]
        for j in range(1, 4):
            dqy_copy(ch, j).start()

    def dq_forward_x(ch):
        for j in range(1, 4):
            dqy_copy(ch, j).wait_recv()
        dqx_copy(ch).start()
        dqc_copy(ch, 0).start()

    def dq_forward_core(ch):
        dqx_copy(ch).wait_recv()
        dqc_copy(ch, 1).start()

    dq_send(0)
    p1_part[:, :, :, pl.ds(0, 256)] = dkacc[...].reshape(NC, 2, R, 256)
    p1_part[:, :, :, pl.ds(256, H)] = (
        dot(dq_own[...], upq[pl.ds(0, H)], 1, 1) + dot(attn[...], odb[...], 1, 1)
    ).reshape(NC, 2, R, H)
    p1_copy = rcopy(p1_part.at[:, 1 - k], p1_pair, grp_s.at[8], grp_r.at[8], mate)
    p1_copy.start()
    sm_own[pl.ds(192, 64)] = dot(bo_all[...], attn[...], 0, 0)[:64]
    all_low = kvl_all[:, :, :, pl.ds(256, 256)].reshape(L, 256)
    sm_own[pl.ds(0, 64)] = dot(all_low, dq_own[...], 0, 0)[:64]
    p1_copy.wait_recv()
    for s in range(NC):
        p1_send[s] = (p1_part[s, k] + p1_pair[s]).astype(BF16)
        to_chip(p1_send, p1_recv, s, 9, s)
    dq_send(1)
    dq_forward_x(0)
    wait_bytes(p1_recv.at[pl.ds(0, NC - 1)], grp_r.at[9])
    total = chip_total(p1_part[c, k] + p1_pair[c], p1_recv)
    piece = pl.ds(pl.multiple_of(f * R, R), R)
    dkey = rotate_back(total[:, :H], cosb[piece], sinb[piece]).astype(BF16)
    dval = total[:, H:256].astype(BF16)
    dkv_all[c, k, :, pl.ds(0, H)] = dkey
    dkv_all[c, k, :, pl.ds(H, H)] = dval
    gather_chips(dkv_all, c, 10)
    p2_all[t, :, pl.ds(0, H)] = total[:, 256:].astype(BF16)
    p2_all[t, :, pl.ds(H, H)] = (
        dot(dkey, upk[pl.ds(H, H)], 1, 1) + dot(dval, upv[pl.ds(H, H)], 1, 1)
    ).astype(BF16)

    @pl.loop(1, NT)
    def _(i):
        rcopy(p2_all.at[t], p2_all.at[t], grp_s.at[12], grp_r.at[12], zdev(i)).start()

    dq_send(2)
    dq_send(3)
    dq_forward_x(1)
    wait_bytes(seven(dkv_all), grp_r.at[10])
    gather_mate(dkv_all, 11).start()
    dq_forward_core(0)
    wait_bytes(p2_all.at[pl.ds(0, NT - 1)], grp_r.at[12])
    total = p2_all[0].astype(F32)
    for i in range(1, NT):
        total = total + p2_all[i].astype(F32)
    back_all[c, k] = total.astype(BF16)
    gather_chips(back_all, c, 13)
    dq_forward_x(2)
    dq_forward_core(1)
    gather_mate(dkv_all, 11).wait_recv()
    for s in range(NT):
        dkv_slot[slot_rows(s)] = dkv_all[block(s)].reshape(T, 256)

    def slots_of(j, way):
        far = ([7, 5, 3, 1], [7, 6, 4, 2])[way]
        return far if j % 2 == way else far[1:]

    def rs_copy(j, way, s):
        send, recv = ((rs_sendr, rs_recvr), (rs_sendl, rs_recvl))[way]
        return rcopy(
            send.at[j, s], recv.at[j, s], rs_s.at[way, j, s], rs_r.at[way, j, s], zdev(1 - 2 * way)
        )

    def rs_step(j, way, s):
        value = zpart[j, slot_rows(slots_of(j, way)[s])]
        send, recv = ((rs_sendr, rs_recvr), (rs_sendl, rs_recvl))[way]
        if s > 0:
            rs_copy(j, way, s - 1).wait_recv()
            value = value + recv[j, s - 1].astype(F32)
        send[j, s] = value.astype(BF16)
        rs_copy(j, way, s).start()

    def z_products(ch):
        rows = pl.ds(*z_chunks[ch])
        dqc_copy(ch, 0).wait_recv()
        dqc_copy(ch, 1).wait_recv()
        dq = jnp.concatenate([dq_all[i // 8, i // 2 % 4, i % 2, rows] for i in range(NF)], axis=1)
        for j in range(4):
            wide = pl.ds(j * 256, 256)
            zpart[j, rows] = dot(dq, wq[wide, :], 1, 1) + dot(dkv_slot[rows], wkv[wide, :], 1, 1)
            for way in range(2):
                s = ch if j % 2 == way else ch - 1
                if s >= 0:
                    rs_step(j, way, s)

    z_products(0)
    dq_forward_x(3)
    wait_bytes(seven(back_all), grp_r.at[13])
    gather_mate(back_all, 14).start()
    gather_mate(back_all, 14).wait_recv()
    for s in range(NT):
        back_slot[slot_rows(s)] = back_all[block(s)].reshape(T, 256)
    halves = []
    for i in range(2):
        rows = pl.ds(i * 128, 128)
        ex_own[rows] = dot(back_slot[:, rows], nb[...], 0, 0).astype(BF16)
        if i == 0:
            ex_own[pl.ds(64, 64)] = dot(back_slot[:, rows], gb[...], 0, 0)[64:].astype(BF16)
        halves.append(rcopy(ex_own.at[rows], ex_recv.at[rows], dp_s.at[1 + i], dp_r.at[1 + i], other))
        halves[i].start()
    z_products(1)
    dq_forward_core(2)
    z_products(2)
    dq_forward_core(3)
    kv_up = dot(all_low, dkv_all[...].reshape(L, 256), 0, 0)
    sm_own[pl.ds(64, 64)] = kv_up[128:192, :H]
    sm_own[pl.ds(128, 64)] = kv_up[192:, H:]
    small = rcopy(sm_own, sm_recv, dp_s.at[0], dp_r.at[0], other)
    small.start()
    z_products(3)

    inverse = column(r_all[t])
    xhat = x_own * inverse
    dhat = []
    for j in range(4):
        wide = pl.ds(j * 256, 256)
        value = zpart[j, slot_rows(0)] + adapter_scale * dot(back_slot[slot_rows(0)], dwt[:, wide], 1, 0)
        for way, recv in enumerate((rs_recvr, rs_recvl)):
            last = len(slots_of(j, way)) - 1
            rs_copy(j, way, last).wait_recv()
            value = value + recv[j, last].astype(F32)
        dhat.append(value)
    dhat = jnp.concatenate(dhat, axis=1) * gain_row()
    inner = dot(ones, dhat * xhat, 1, 1, precision=lax.Precision.HIGHEST)
    ip_own[...] = jnp.concatenate([inner, inner], axis=1)

    @pl.loop(1, NF)
    def _(i):
        rcopy(ip_own, ip_recv.at[i - 1], grp_s.at[15], grp_r.at[15], fdev(i)).start()

    small.wait_recv()
    both = adapter_scale * (sm_own[...] + sm_recv[...])
    sm_o[pl.ds(0, 64)] = both[:64]
    sm_o[pl.ds(64, 64, stride=2)] = both[64:128]
    sm_o[pl.ds(65, 64, stride=2)] = both[128:192]
    sm_o[pl.ds(192, 64)] = both[192:]
    wait_bytes(ip_recv, grp_r.at[15])
    inner = total_f(ip_own[...], ip_recv) / (W * NF)
    hid_o[...] = gb[slot_rows(0)].astype(F32) + inverse * (dhat - xhat * column(inner))
    halves[0].wait_recv()

    def added(i, n):
        return adapter_scale * (ex_own[pl.ds(i, n)].astype(F32) + ex_recv[pl.ds(i, n)].astype(F32))

    pd_o[pl.ds(0, 64)] = added(0, 64)
    ou_o[...] = added(64, 64)
    halves[1].wait_recv()
    pd_o[pl.ds(64, 128)] = added(128, 128)

    g_finish()
    x_finish()
    a_finish()
    q_finish()
    for ch in range(4):
        kvl_copy(ch).wait_send()
        dqx_copy(ch).wait_send()
        dqc_copy(ch, 0).wait_send()
        dqc_copy(ch, 1).wait_send()
        for j in range(1, 4):
            dqy_copy(ch, j).wait_send()
    for j in range(4):
        for way in range(2):
            for s in range(len(slots_of(j, way))):
                rs_copy(j, way, s).wait_send()
    p1_copy.wait_send()
    small.wait_send()
    for half in halves:
        half.wait_send()
    gather_mate(kvl_all, 7).wait_send()
    gather_mate(dkv_all, 11).wait_send()
    gather_mate(back_all, 14).wait_send()
    sent = {
        0: ss_recv, 1: r_all.at[pl.ds(0, NT - 1)], 2: bo_recv, 3: bo_all.at[pl.ds(0, (NF - 1) * R)],
        5: kvl_recv.at[pl.ds(0, NC - 1)], 6: seven(kvl_all), 9: p1_recv.at[pl.ds(0, NC - 1)], 10: seven(dkv_all),
        12: p2_all.at[pl.ds(0, NT - 1)], 13: seven(back_all), 15: ip_recv,
    }
    for n, ref in sent.items():
        wait_bytes(ref, grp_s.at[n])


def hand_over(hid, pd, ou, sm, hid_o, pd_o, ou_o, qu_o, ku_o, od_o):
    hid_o[...] = hid[...]
    pd_o[...] = pd[...]
    ou_o[...] = ou[...]
    qu_o[...] = sm[pl.ds(0, 64)]
    ku_o[...] = sm[pl.ds(64, 128)]
    od_o[...] = sm[pl.ds(192, 64)]


def local(
    residual_input,
    block_output_gradient,
    norm_gain_vector,
    query_matrix,
    keyvalue_matrix,
    output_matrix,
    adapter_projection_down,
    adapter_query_up,
    adapter_keyvalue_up,
    adapter_output_down,
    adapter_output_up,
):
    cosine, sine = rope_tables()
    vm = pltpu.VMEM
    dma = pltpu.SemaphoreType.DMA
    quarter = [vm((4, L, H), BF16)] * 7 + [vm((3, L, H), BF16)]
    heads = [vm((4, L, H), F32)] * 2 + quarter
    scratch = [
        vm((L, W), BF16), vm((L, W), BF16), vm((L, W), BF16),
        vm((W, 2048), BF16), vm((2048, W), BF16), vm((W, 256), BF16), vm((256, W), BF16), vm((128, W), BF16),
        vm((256, H), BF16), vm((256, H), BF16), vm((256, H), BF16), vm((128, H), BF16), vm((128, H), BF16),
        vm((8, H), F32), vm((L, H), F32), vm((L, H), F32),
        vm((2 * W, H), BF16), vm((2 * W, H), F32), vm((128, H), BF16), vm((128, H), F32),
        vm((8, H), F32), vm((NF - 1, 8, H), F32), vm((NT, 8, H), F32), vm((8, H), F32), vm((NF - 1, 8, H), F32),
        vm((L, H), BF16), vm((NF - 1, R, H), BF16), vm((L, H), BF16),
        vm((NC, 2, R, 512), F32), vm((NC, R, 512), F32), vm((NC, R, 512), F32), vm((NC, R, 512), F32),
        vm((NC, 2, R, 512), BF16),
        *heads, *heads,
        vm((L, H), BF16), vm((L, H), BF16), vm((L, H), BF16), vm((L, H), BF16), vm((2, 4, 2, L, H), BF16),
        vm((L, 256), F32),
        vm((NC, 2, R, 384), F32), vm((NC, R, 384), F32), vm((NC, R, 384), BF16), vm((NC, R, 384), BF16),
        vm((NC, 2, R, 256), BF16), vm((L, 256), BF16), vm((NT, R, 256), BF16),
        vm((NC, 2, R, 256), BF16), vm((L, 256), BF16),
        vm((4, L, 256), F32),
        vm((4, 4, T, 256), BF16), vm((4, 4, T, 256), BF16), vm((4, 4, T, 256), BF16), vm((4, 4, T, 256), BF16),
        vm((256, H), F32), vm((256, H), F32), vm((256, W), BF16), vm((256, W), BF16),
        dma((16,)), dma((16,)), dma((16,)), dma((2, 2, 4)), dma((2, 2, 4)), dma((4,)), dma((4,)),
        dma((2, 5, 2)), dma((2, 5, 2)), dma((2, 5)), dma((2, 5)), dma((2, 5, 3)), dma((2, 5, 3)),
        dma((4, 3)), dma((4, 3)), dma((4,)), dma((4,)), dma((4, 2)), dma((4, 2)),
        dma((2, 4, 4)), dma((2, 4, 4)), dma((3,)), dma((3,)),
    ]
    hidden, down, up, small = pl.pallas_call(
        kernel,
        out_shape=(
            jax.ShapeDtypeStruct((T, W), F32),
            jax.ShapeDtypeStruct((192, W), F32),
            jax.ShapeDtypeStruct((64, W), F32),
            jax.ShapeDtypeStruct((256, H), F32),
        ),
        in_specs=[pl.BlockSpec(memory_space=pl.ANY)] * 13,
        out_specs=(pl.BlockSpec(memory_space=pltpu.VMEM),) * 4,
        scratch_shapes=scratch,
        compiler_params=pltpu.CompilerParams(
            collective_id=0, has_side_effects=True, vmem_limit_bytes=60 * 2**20
        ),
        name="adapter_backward",
    )(
        residual_input[0],
        block_output_gradient[0],
        norm_gain_vector.reshape(8, H),
        query_matrix[:, 0, :],
        output_matrix[0],
        keyvalue_matrix.reshape(2 * W, H),
        adapter_projection_down.T,
        adapter_output_up,
        adapter_query_up[:, 0, :],
        adapter_keyvalue_up.reshape(128, H),
        adapter_output_down[0].T,
        jnp.asarray(cosine),
        jnp.asarray(sine),
    )
    hidden, down, up, query_up, keyvalue_up, output_down = pl.pallas_call(
        hand_over,
        out_shape=(
            jax.ShapeDtypeStruct((T, W), F32),
            jax.ShapeDtypeStruct((192, W), F32),
            jax.ShapeDtypeStruct((64, W), F32),
            jax.ShapeDtypeStruct((64, H), F32),
            jax.ShapeDtypeStruct((128, H), F32),
            jax.ShapeDtypeStruct((64, H), F32),
        ),
        in_specs=[pl.BlockSpec(memory_space=pltpu.VMEM)] * 4,
        out_specs=(pl.BlockSpec(memory_space=pltpu.VMEM),) * 6,
        name="hand_over",
    )(hidden, down, up, small)
    return (
        hidden[None],
        down.T,
        query_up[:, None, :],
        keyvalue_up.reshape(64, 2, H),
        output_down.T[None],
        up,
    )


def solution(mesh):
    in_specs = (
        P("dp", "tensor", "fsdp"),
        P("dp", "tensor", "fsdp"),
        P("fsdp"),
        P("fsdp", "tensor", None),
        P("fsdp", None, "tensor"),
        P("tensor", None, "fsdp"),
        P("fsdp", None),
        P(None, "tensor", "fsdp"),
        P(None, None, "tensor"),
        P("tensor", "fsdp", None),
        P(None, "fsdp"),
    )
    out_specs = (
        P("dp", "tensor", "fsdp"),
        P("fsdp", None),
        P(None, "tensor", "fsdp"),
        P(None, None, "tensor"),
        P("tensor", "fsdp", None),
        P(None, "fsdp"),
    )
    return jax.shard_map(local, mesh=mesh, in_specs=in_specs, out_specs=out_specs, check_vma=False)
```
